512 devices in a mesh: section: 4 (over y), seq: 128 (over x, z, core).
Axes of the slice: x: 4, y: 4, z: 16, core: 2. Of those that a mesh axis runs over, the one named last changes fastest.
Arguments:
- tokens: bfloat16 [32768, 2560], P('seq'), may hold values from -6 to 6
- w_query: bfloat16 [2560, 2560], P('seq', 'section'), may hold values from -0.125 to 0.125
- w_key: bfloat16 [2560, 2560], P('seq', 'section'), may hold values from -0.125 to 0.125
- w_value: bfloat16 [2560, 2560], P('seq', 'section'), may hold values from -0.125 to 0.125
- gain: bfloat16 [2560], P('section'), may hold values from 0.099609375 to 1.8984375
- w_out: bfloat16 [2560, 2560], P('section'), may hold values from -0.125 to 0.125
Outputs:
- hidden_out: bfloat16 [32768, 2560], P('seq', 'section')
The draws below stay inside these ranges and needn't reach their ends.
All inputs are finite; a program needn't handle non-finite values.
Results may differ from the reference program's by a relative error of at most 0.015.
Values may be sent and summed in bfloat16 or wider, within the bound.
A program may use at most 128 MiB of HBM per device.

```python
import jax
import jax.numpy as jnp
from jax import lax

H = 20
E = 128
SPAN = 256
TOKENS = 32768
D = 2560


def level_of(own_key, extent, split, smallest, largest):
    level, own = 1.0, jax.random.fold_in(own_key, 6)
    for axis_at, parts in split:
        steps = jnp.exp(jax.random.uniform(jax.random.fold_in(own, axis_at), (parts,), jnp.float32, smallest / len(split), largest / len(split)))
        level = level * jnp.repeat(steps, extent[axis_at] // parts).reshape([-1 if axis == axis_at else 1 for axis in range(len(extent))])
    return level


def scatter_about(stream_key, extent, scale, bound, split=(), held_as=jnp.bfloat16):
    factor_of = level_of(stream_key, extent, split, -0.22, 0.18) if split else 1.0
    result = jax.random.normal(stream_key, extent, jnp.float32) * scale * factor_of
    return jnp.minimum(jnp.maximum(result, -bound), bound).astype(held_as)


def setup_inputs(seed: int = 0) -> dict:
    streams_of = jax.random.split(jax.random.key(seed), 7)
    tokens = scatter_about(streams_of[0], (TOKENS, D), 1.0, 6.0, ((0, 128),))
    w_query = scatter_about(streams_of[1], (D, H * E), D ** -0.5, 0.125, ((0, 128), (1, 4)))
    w_key = scatter_about(streams_of[2], (D, H * E), D ** -0.5, 0.125, ((0, 128), (1, 4)))
    w_value = scatter_about(streams_of[3], (D, H * E), D ** -0.5, 0.125, ((0, 128), (1, 4)))
    gain = jnp.clip(1.0 + 0.18 * jax.random.normal(streams_of[4], (H * E,), jnp.float32), 0.099609375, 1.8984375).astype(jnp.bfloat16)
    w_out = scatter_about(streams_of[5], (H * E, D), (H * E) ** -0.5, 0.125, ((0, 4),))
    return {"tokens": tokens, "w_query": w_query, "w_key": w_key, "w_value": w_value, "gain": gain, "w_out": w_out}


def reference(tokens, w_query, w_key, w_value, gain, w_out):
    blocks = TOKENS // SPAN
    queries = jax.nn.silu(jnp.dot(tokens, w_query, preferred_element_type=jnp.float32)).astype(jnp.bfloat16)
    key_rows = jax.nn.silu(jnp.dot(tokens, w_key, preferred_element_type=jnp.float32)).astype(jnp.bfloat16)
    value_rows = jnp.dot(tokens, w_value, preferred_element_type=jnp.float32).astype(jnp.bfloat16)
    causal = jnp.arange(SPAN)[:, None] >= jnp.arange(SPAN)[None, :]

    def one_head(head_index):
        first_col = (head_index * E).astype(jnp.int32)
        query_head = lax.dynamic_slice_in_dim(queries, first_col, E, 1).astype(jnp.float32).reshape(blocks, SPAN, E)
        key_head = lax.dynamic_slice_in_dim(key_rows, first_col, E, 1).astype(jnp.float32).reshape(blocks, SPAN, E)
        value_head = lax.dynamic_slice_in_dim(value_rows, first_col, E, 1).astype(jnp.float32).reshape(blocks, SPAN, E)
        scores = jnp.einsum('ncf,ndf->ncd', query_head, key_head)
        scores = jnp.where(causal[None], scores, 0.0).astype(jnp.bfloat16)
        scores = lax.optimization_barrier(scores).astype(jnp.float32)
        local_part = jnp.einsum('ncd,ndf->ncf', scores, value_head)
        block_state = jnp.einsum('ncf,ncg->nfg', key_head, value_head)
        running = jnp.cumsum(block_state, axis=0)[:-1]
        prefix = jnp.concatenate([jnp.zeros_like(block_state[:1]), running], axis=0)
        prefix_b = lax.optimization_barrier(prefix.astype(jnp.bfloat16)).astype(jnp.float32)
        carried = jnp.einsum('ncf,nfg->ncg', query_head, prefix_b)
        return (carried + local_part).reshape(TOKENS, E)
    combined = lax.map(one_head, jnp.arange(H, dtype=jnp.int32))
    scale_rows = gain.astype(jnp.float32).reshape(H, 1, E)
    normed = combined * lax.rsqrt(lax.optimization_barrier(jnp.mean(combined * combined, axis=-1, keepdims=True)) + 1e-05) * scale_rows
    attended = jnp.transpose(normed, (1, 0, 2)).reshape(TOKENS, H * E).astype(jnp.bfloat16)
    projected = jnp.dot(attended, w_out, preferred_element_type=jnp.float32)
    return (tokens.astype(jnp.float32) + projected).astype(jnp.bfloat16)
```

```python
import jax
import jax.numpy as jnp
from jax import lax
from jax.experimental import pallas as pl
from jax.experimental.pallas import tpu as pltpu
from jax.sharding import PartitionSpec as P

E = 128
X, Z, Y = 4, 16, 4
HALF = Z // 2
ROWS = 20
HEADS = 5
COLS = 3 * HEADS
TILES = COLS + 4
CUT = 7
SPAN = 256
OWNERS, SHARE = 10, 2
MESH = pl.DeviceIdType.MESH
BF = jnp.bfloat16
F32 = jnp.float32


def dot(a, b):
    return jnp.dot(a, b, preferred_element_type=F32)


def kernel(
    tokens, wq, wk, wv, gain, w_out, out,
    G, T1, T2, PB, acc, wo, kvq, local, att,
    state, sib_state, chip_sum, zin, xout, xin, pout, pin, pfull,
    axs, axr, azs, azr, bzs, bzr, bxs, bxr, sas, sar, sbs, sbr,
    ws, wr, vs, vr, wl, ps, pr, z1s, z1r, xs, xr, z2s, z2r, qs, qr, ats, atr,
):
    seq = lax.axis_index("seq")
    y = lax.axis_index("section")
    c = lax.rem(seq, 2)
    z = lax.rem(lax.div(seq, 2), Z)
    x = lax.div(seq, 2 * Z)

    def at(dx=0, dy=0, dz=0, core=None):
        core = c if core is None else core
        nx, ny, nz = lax.rem(x + dx + X, X), lax.rem(y + dy + Y, Y), lax.rem(z + dz + Z, Z)
        return (ny, (nx * Z + nz) * 2 + core)

    def zz(d):
        return lax.rem(z + d + Z, Z)

    def rcopy(src, dst, ssem, rsem, dev):
        return pltpu.make_async_remote_copy(
            src_ref=src, dst_ref=dst, send_sem=ssem, recv_sem=rsem,
            device_id=dev, device_id_type=MESH,
        )

    sibling = at(core=1 - c)

    weights = (wk, wv, wq)
    for t in range(COLS):
        G[c, z, x, t] = weights[t // HEADS][0:16, pl.ds((t % HEADS) * E, E)]
    for u in range(4):
        parts = []
        for j in range(4):
            t = 4 * u + j
            if t < COLS:
                parts.append(weights[t // HEADS][16:20, pl.ds((t % HEADS) * E, E)].astype(F32))
            else:
                parts.append(jnp.zeros((4, E), F32))
        G[c, z, x, COLS + u] = jnp.concatenate(parts, axis=0).astype(BF)

    barrier = pltpu.get_barrier_semaphore()
    near = [at(dz=1), at(dz=-1), at(dx=1), at(dx=-1), at(dx=2), sibling, at(dy=1), at(dy=-1), at(dy=2)]
    for dev in near:
        pl.semaphore_signal(barrier, inc=1, device_id=dev, device_id_type=MESH)
    pl.semaphore_wait(barrier, len(near))

    XD = (1, -1, 2)

    def a_x(k):
        ref = G.at[c, z, x, pl.ds(0, CUT)]
        return rcopy(ref, ref, axs.at[k], axr.at[k], at(dx=XD[k]))

    def a_z(way, step, block, dz):
        ref = G.at[c, block, :, pl.ds(0, CUT)]
        return rcopy(ref, ref, azs.at[way, step], azr.at[way, step], at(dz=dz))

    def b_z(way, step, block, dz):
        ref = G.at[c, block, x, pl.ds(CUT, TILES - CUT)]
        return rcopy(ref, ref, bzs.at[way, step], bzr.at[way, step], at(dz=dz))

    def b_x(n, block, k):
        ref = G.at[c, block, x, pl.ds(CUT, TILES - CUT)]
        return rcopy(ref, ref, bxs.at[n, k], bxr.at[n, k], at(dx=XD[k]))

    def s_a(n, block):
        ref = G.at[c, block, :, pl.ds(0, CUT)]
        return rcopy(ref, ref, sas.at[n], sar.at[n], sibling)

    def s_b(n, block):
        ref = G.at[c, block, :, pl.ds(CUT, TILES - CUT)]
        return rcopy(ref, ref, sbs.at[n], sbr.at[n], sibling)

    def block_of(n):
        if n == 0:
            return z
        if n == Z - 1:
            return zz(HALF)
        return zz(-((n + 1) // 2)) if n % 2 else zz(n // 2)

    def blocks_at(step):
        return [0] if step == 0 else ([Z - 1] if step == HALF else [2 * step - 1, 2 * step])

    def w_y(k):
        dev = at(dy=XD[k])
        return rcopy(
            w_out.at[pl.ds(320 * c, 320), pl.ds(pl.multiple_of(640 * dev[0], 128), 640)],
            wo.at[y, pl.ds(320 * c, 320)], ws.at[k], wr.at[k], dev,
        )

    def w_s(k):
        ref = wo.at[lax.rem(y - XD[k] + Y, Y), pl.ds(320 * c, 320)]
        return rcopy(ref, ref, vs.at[k], vr.at[k], sibling)

    def w_own():
        return pltpu.make_async_copy(
            w_out.at[:, pl.ds(pl.multiple_of(640 * y, 128), 640)], wo.at[y], wl
        )

    for k in range(3):
        a_x(k).start()
    b_z(0, 0, z, 1).start()
    b_z(1, 0, z, -1).start()
    for k in range(3):
        b_x(0, z, k).start()
    for k in range(3):
        w_y(k).start()
    w_own().start()

    PB[...] = jnp.zeros_like(PB)
    row = lax.broadcasted_iota(jnp.int32, (80, 256), 0)
    lane = lax.broadcasted_iota(jnp.int32, (80, 256), 1)
    base = (lane >> 7) * 40 + ((lane >> 6) & 1) * 20
    r16 = lane & 15
    for xx in range(X):
        here = ((lane >> 4) & 3) == xx
        PB[0, xx, 176:256] = jnp.where(here & (row == base + r16), 1.0, 0.0).astype(BF)
        PB[1, xx, 176:256] = jnp.where(here & (row == base + 16 + (r16 & 3)), 1.0, 0.0).astype(BF)
    acc[...] = jnp.zeros_like(acc)

    lane_j = (lax.broadcasted_iota(jnp.int32, (SPAN, E), 1) & 15) >> 2

    def arrange(m, _):
        window = jnp.minimum(lax.div(80 * m, 128), 3)
        off = pl.multiple_of(176 - (80 * m - 128 * window), 16)
        lhs = jnp.concatenate(
            [tokens[:, pl.ds(pl.multiple_of(640 * xx + 128 * window, 128), 256)] for xx in range(X)], axis=1
        )
        first = dot(lhs, jnp.concatenate([PB[0, xx, pl.ds(off, 256)] for xx in range(X)], axis=0)).astype(BF)
        rest = dot(lhs, jnp.concatenate([PB[1, xx, pl.ds(off, 256)] for xx in range(X)], axis=0))
        for half in range(2):
            T1[2 * m + half] = first[:, half * E:(half + 1) * E]
            part = rest[:, half * E:(half + 1) * E]
            for j in range(4):
                T2[j, 2 * m + half] = jnp.where(lane_j == j, part, 0.0).astype(BF)
        return 0

    lax.fori_loop(0, Z // 2, arrange, 0)

    def multiply(z1, z2):
        def pair(p, _):
            h, j = lax.div(p, 4), lax.rem(p, 4)
            lhs = jnp.concatenate([T1[z1], T1[z2], T2[j, z1], T2[j, z2]], axis=1)

            def block(t):
                return jnp.concatenate([G[:, z1, :, t].reshape(E, E), G[:, z2, :, t].reshape(E, E)], axis=0)

            t1, t2 = 8 * h + j, 8 * h + 4 + j
            u1, u2 = COLS + 2 * h, COLS + 2 * h + 1
            rhs = jnp.concatenate(
                [jnp.concatenate([block(t1), block(t2)], axis=1), jnp.concatenate([block(u1), block(u2)], axis=1)],
                axis=0,
            )
            acc[p] += dot(lhs, rhs)
            return 0

        lax.fori_loop(0, 8, pair, 0)

    def sibling_b(step):
        for n in blocks_at(step):
            for k in range(3):
                b_x(n, block_of(n), k).wait_recv()
            s_b(n, block_of(n)).start()

    def consume(step):
        for n in blocks_at(step):
            s_a(n, block_of(n)).wait_recv()
            s_b(n, block_of(n)).wait_recv()

    def multiply_step(step):
        consume(step)
        if step == HALF:
            multiply(z, zz(HALF))
        elif step > 0:
            multiply(zz(-step), zz(step))

    for k in range(3):
        a_x(k).wait_recv()
    a_z(0, 0, z, 1).start()
    a_z(1, 0, z, -1).start()
    s_a(0, z).start()

    way = 1 - 2 * c
    for step in range(1, HALF):
        last = step == HALF - 1
        minus, plus = zz(-step), zz(step)
        b_z(0, step - 1, minus, 1).wait_recv()
        if not last:
            b_z(0, step, minus, 1).start()
        b_z(1, step - 1, plus, -1).wait_recv()
        if not last:
            b_z(1, step, plus, -1).start()
        else:
            b_z(c, step, zz(-step * way), way).start()
        for n, block in zip(blocks_at(step), (minus, plus)):
            for k in range(3):
                b_x(n, block, k).start()
        a_z(0, step - 1, minus, 1).wait_recv()
        if not last:
            a_z(0, step, minus, 1).start()
        a_z(1, step - 1, plus, -1).wait_recv()
        if not last:
            a_z(1, step, plus, -1).start()
        else:
            a_z(c, step, zz(-step * way), way).start()
        for n, block in zip(blocks_at(step), (minus, plus)):
            s_a(n, block).start()
        sibling_b(step - 1)
        if step >= 2:
            multiply_step(step - 2)
        if step == 4:
            for k in range(3):
                w_y(k).wait_recv()
                w_s(k).start()
            w_own().wait()

    far = zz(HALF)
    b_z(c, HALF - 1, far, way).wait_recv()
    for k in range(3):
        b_x(Z - 1, far, k).start()
    a_z(c, HALF - 1, far, way).wait_recv()
    s_a(Z - 1, far).start()
    sibling_b(HALF - 1)
    multiply_step(HALF - 2)
    sibling_b(HALF)
    multiply_step(HALF - 1)
    multiply_step(HALF)

    def tile(t):
        p, half = (t // 8) * 4 + t % 4, (t % 8) // 4
        return acc[p, :, half * E:(half + 1) * E]

    def silu(v):
        return v / (1.0 + jnp.exp(-v))

    for h in range(HEADS):
        kvq[h] = silu(tile(h)).astype(BF)
        kvq[HEADS + h] = tile(HEADS + h).astype(BF)
        s = lax.dot_general(kvq[h], kvq[HEADS + h], (((0,), (0,)), ((), ())), preferred_element_type=F32)
        state[pl.ds(8 * h, 8)] = s.astype(BF).reshape(8, 16, E)
    pair1 = rcopy(state, sib_state, ps, pr, sibling)
    pair1.start()
    for h in range(HEADS):
        kvq[2 * HEADS + h] = silu(tile(2 * HEADS + h)).astype(BF)
    pair1.wait_recv()
    mine = pl.ds(20 * c, 20)
    chip_sum[...] = (state[mine].astype(F32) + sib_state[mine].astype(F32)).astype(BF)

    def owner_z(i):
        return (i * Z) // OWNERS

    def z1(i):
        dst = owner_z(i)
        return rcopy(
            chip_sum.at[pl.ds(SHARE * i, SHARE)], zin.at[z], z1s.at[i], z1r.at[z],
            (y, (x * Z + dst) * 2 + c),
        )

    my_i = lax.div(z * OWNERS + Z - 1, Z)
    is_owner = lax.div(my_i * Z, OWNERS) == z
    for i in range(OWNERS):
        @pl.when(z != owner_z(i))
        def _():
            z1(i).start()

        @pl.when(z == owner_z(i))
        def _():
            zin[z] = chip_sum[pl.ds(SHARE * i, SHARE)]

    causal = lax.broadcasted_iota(jnp.int32, (SPAN, SPAN), 0) >= lax.broadcasted_iota(jnp.int32, (SPAN, SPAN), 1)
    for h in range(HEADS):
        q, k, v = kvq[2 * HEADS + h], kvq[h], kvq[HEADS + h]
        scores = lax.dot_general(q, k, (((1,), (1,)), ((), ())), preferred_element_type=F32)
        local[h] = dot(jnp.where(causal, scores, 0.0).astype(BF), v)

    def x_copy(k):
        return rcopy(xout, xin.at[x], xs.at[k], xr.at[k], at(dx=XD[k]))

    def z1_in(src):
        return rcopy(chip_sum.at[pl.ds(0, SHARE)], zin.at[src], z1s.at[0], z1r.at[src], sibling)

    def z2(dst):
        return rcopy(
            pout.at[dst], pin.at[pl.ds(SHARE * my_i, SHARE)], z2s.at[dst], z2r.at[my_i],
            (y, (x * Z + dst) * 2 + c),
        )

    def z2_in(i):
        return rcopy(pout.at[0], pin.at[pl.ds(SHARE * i, SHARE)], z2s.at[0], z2r.at[i], sibling)

    @pl.when(is_owner)
    def _():
        for src in range(Z):
            @pl.when(src != z)
            def _():
                z1_in(src).wait_recv()
        total = jnp.zeros((SHARE, 16, E), F32)
        for src in range(Z):
            total = total + zin[src].astype(F32)
        xout[...] = total
        for k in range(3):
            x_copy(k).start()
        for k in range(3):
            x_copy(k).wait_recv()
        running = jnp.zeros((SHARE, 16, E), F32)
        for src in range(X):
            running = running + jnp.where((src < x), xin[src], 0.0)
        for dst in range(Z):
            pout[dst] = running.astype(BF)
            running = running + zin[dst].astype(F32)

            @pl.when(dst != z)
            def _():
                z2(dst).start()
        pin[pl.ds(SHARE * my_i, SHARE)] = pout[z]

    for i in range(OWNERS):
        @pl.when(z != owner_z(i))
        def _():
            z2_in(i).wait_recv()
    pair2 = rcopy(pin, pfull.at[pl.ds(20 * c, 20)], qs, qr, sibling)
    pair2.start()
    pfull[mine] = pin[...]
    pair2.wait_recv()

    def a_y(k, h):
        return rcopy(att.at[y, h], att.at[y, h], ats.at[k, h], atr.at[k, h], at(dy=XD[k]))

    for h in range(HEADS):
        before = pfull[pl.ds(8 * h, 8)].reshape(E, E).astype(F32)
        first = sib_state[pl.ds(8 * h, 8)].reshape(E, E).astype(F32)
        prefix = jnp.where(c == 1, before + first, before).astype(BF)
        combined = dot(kvq[2 * HEADS + h], prefix) + local[h]
        scale = lax.rsqrt(jnp.mean(combined * combined, axis=-1, keepdims=True) + 1e-05)
        att[y, h] = (combined * scale * gain[h:h + 1].astype(F32)).astype(BF)
        for k in range(3):
            a_y(k, h).start()

    def project(section):
        lhs = jnp.concatenate([att[section, h] for h in range(HEADS)], axis=1)
        return dot(lhs, wo[section])

    for k in range(3):
        w_s(k).wait_recv()
    total = tokens[:, pl.ds(pl.multiple_of(640 * y, 128), 640)].astype(F32) + project(y)

    for k in range(3):
        a_x(k).wait_send()
        w_y(k).wait_send()
        w_s(k).wait_send()
    for step in range(HALF - 1):
        for w, dz in ((0, 1), (1, -1)):
            a_z(w, step, z, dz).wait_send()
            b_z(w, step, z, dz).wait_send()
    a_z(c, HALF - 1, z, way).wait_send()
    b_z(c, HALF - 1, z, way).wait_send()
    for n in range(Z):
        s_a(n, z).wait_send()
        s_b(n, z).wait_send()
        for k in range(3):
            b_x(n, z, k).wait_send()
    pair1.wait_send()
    pair2.wait_send()
    for i in range(OWNERS):
        @pl.when(z != owner_z(i))
        def _():
            z1(i).wait_send()

    @pl.when(is_owner)
    def _():
        for k in range(3):
            x_copy(k).wait_send()
        for dst in range(Z):
            @pl.when(dst != z)
            def _():
                z2(dst).wait_send()

    for k in range(3):
        for h in range(HEADS):
            a_y(k, h).wait_recv()
        total = total + project(lax.rem(y - XD[k] + Y, Y))
    out[...] = total.astype(BF)
    for k in range(3):
        for h in range(HEADS):
            a_y(k, h).wait_send()


def on_device(tokens, w_query, w_key, w_value, gain, w_out):
    vmem = pl.BlockSpec(memory_space=pltpu.VMEM)
    dma = pltpu.SemaphoreType.DMA
    return pl.pallas_call(
        kernel,
        name="layer",
        out_shape=jax.ShapeDtypeStruct((SPAN, 640), BF),
        in_specs=[vmem, vmem, vmem, vmem, vmem, pl.BlockSpec(memory_space=pl.ANY)],
        out_specs=vmem,
        scratch_shapes=[
            pltpu.VMEM((2, Z, X, TILES, 16, E), BF),
            pltpu.VMEM((Z, SPAN, E), BF),
            pltpu.VMEM((4, Z, SPAN, E), BF),
            pltpu.VMEM((2, X, 432, 256), BF),
            pltpu.VMEM((8, SPAN, 256), F32),
            pltpu.VMEM((Y, 640, 640), BF),
            pltpu.VMEM((COLS, SPAN, E), BF),
            pltpu.VMEM((HEADS, SPAN, E), F32),
            pltpu.VMEM((Y, HEADS, SPAN, E), BF),
            pltpu.VMEM((40, 16, E), BF),
            pltpu.VMEM((40, 16, E), BF),
            pltpu.VMEM((20, 16, E), BF),
            pltpu.VMEM((Z, SHARE, 16, E), BF),
            pltpu.VMEM((SHARE, 16, E), F32),
            pltpu.VMEM((X, SHARE, 16, E), F32),
            pltpu.VMEM((Z, SHARE, 16, E), BF),
            pltpu.VMEM((20, 16, E), BF),
            pltpu.VMEM((40, 16, E), BF),
            dma((3,)), dma((3,)),
            dma((2, HALF)), dma((2, HALF)),
            dma((2, HALF)), dma((2, HALF)),
            dma((Z, 3)), dma((Z, 3)),
            dma((Z,)), dma((Z,)), dma((Z,)), dma((Z,)),
            dma((3,)), dma((3,)), dma((3,)), dma((3,)), dma(()),
            dma(()), dma(()),
            dma((OWNERS,)), dma((Z,)),
            dma((3,)), dma((3,)),
            dma((Z,)), dma((OWNERS,)),
            dma(()), dma(()),
            dma((3, HEADS)), dma((3, HEADS)),
        ],
        compiler_params=pltpu.CompilerParams(
            collective_id=1, has_side_effects=True, vmem_limit_bytes=56 << 20
        ),
    )(tokens, w_query, w_key, w_value, gain.reshape(HEADS, E), w_out)


def solution(mesh):
    placed = (
        P("seq", None),
        P("seq", "section"),
        P("seq", "section"),
        P("seq", "section"),
        P("section"),
        P("section", None),
    )
    return jax.shard_map(
        on_device, mesh=mesh, in_specs=placed, out_specs=P("seq", "section"), check_vma=False
    )
```

```python
import jax
import jax.numpy as jnp
from jax import lax
from jax.experimental import pallas as pl
from jax.experimental.pallas import tpu as pltpu
from jax.sharding import PartitionSpec as P

E = 128
X, Z, Y = 4, 16, 4
ROWS = 20
HEADS = 5
COLS = 3 * HEADS
FIRST = (0, 2 * HEADS)
WIDE = (2 * HEADS, HEADS)
TILES = (13, 7)
CUT = (3, 2)
SPAN = 256
OWNERS, SHARE = 10, 2
MESH = pl.DeviceIdType.MESH
BF = jnp.bfloat16
F32 = jnp.float32


def dot(a, b):
    return jnp.dot(a, b, preferred_element_type=F32)


def kernel(
    tokens_hbm, wq, wk, wv, gain, w_out, out, tokens,
    G0, G1, T1, T2, PB, acc, wo, kvq, local, att,
    state, sib_state, chip_sum, zin, xout, xin, pout, pin, pfull,
    axs, axr, azs, azr, bzs, bzr, bxs, bxr, ss, sr,
    ws, wr, vs, vr, wl, ps, pr, z1s, z1r, xs, xr, z2s, z2r, qs, qr, ats, atr, tl,
):
    seq = lax.axis_index("seq")
    y = lax.axis_index("section")
    c = lax.rem(seq, 2)
    z = lax.rem(lax.div(seq, 2), Z)
    x = lax.div(seq, 2 * Z)

    def at(dx=0, dy=0, dz=0, core=None):
        core = c if core is None else core
        nx, ny, nz = lax.rem(x + dx + X, X), lax.rem(y + dy + Y, Y), lax.rem(z + dz + Z, Z)
        return (ny, (nx * Z + nz) * 2 + core)

    def zz(d):
        return lax.rem(z + d + Z, Z)

    def rcopy(src, dst, ssem, rsem, dev):
        return pltpu.make_async_remote_copy(
            src_ref=src, dst_ref=dst, send_sem=ssem, recv_sem=rsem,
            device_id=dev, device_id_type=MESH,
        )

    sibling = at(core=1 - c)

    way = 1 - 2 * c
    G = (G0, G1)

    barrier = pltpu.get_barrier_semaphore()
    greeted = [at(dz=d) for d in (1, -1, 2, -2, 3, -3)] + [at(dx=1), at(dx=-1), at(dx=2), sibling]
    greeted += [at(dy=1), at(dy=-1), at(dy=2)]
    for dev in greeted:
        pl.semaphore_signal(barrier, inc=1, device_id=dev, device_id_type=MESH)
    fetch = pltpu.make_async_copy(tokens_hbm, tokens, tl)
    fetch.start()

    weights = (wk, wv, wq)
    for ph in range(2):
        for i in range(WIDE[ph]):
            t = FIRST[ph] + i
            G[ph][c, z, x, i] = weights[t // HEADS][0:16, pl.ds((t % HEADS) * E, E)]
        for u in range(TILES[ph] - WIDE[ph]):
            parts = []
            for i in range(4 * u, 4 * u + 4):
                t = FIRST[ph] + i
                if i < WIDE[ph]:
                    parts.append(weights[t // HEADS][16:20, pl.ds((t % HEADS) * E, E)].astype(F32))
                else:
                    parts.append(jnp.zeros((4, E), F32))
            G[ph][c, z, x, WIDE[ph] + u] = jnp.concatenate(parts, axis=0).astype(BF)

    pl.semaphore_wait(barrier, len(greeted))

    XD = (1, -1, 2)

    def place(d):
        return (d + 7) % Z

    def part_a(ph):
        return pl.ds(0, CUT[ph])

    def part_b(ph):
        return pl.ds(CUT[ph], TILES[ph] - CUT[ph])

    def a_x(ph, k):
        ref = G[ph].at[c, z, x, part_a(ph)]
        return rcopy(ref, ref, axs.at[ph], axr.at[ph], at(dx=XD[k]))

    def a_x_in(ph):
        ref = G[ph].at[c, z, pl.ds(0, 3), part_a(ph)]
        return rcopy(ref, ref, axs.at[ph], axr.at[ph], sibling)

    def a_z(ph, d, delta):
        ref = G[ph].at[c, zz(d), :, part_a(ph)]
        return rcopy(ref, ref, azs.at[ph], azr.at[ph, place(d - delta)], at(dz=delta))

    def b_z(ph, d, delta):
        ref = G[ph].at[c, zz(d), x, part_b(ph)]
        return rcopy(ref, ref, bzs.at[ph], bzr.at[ph, place(d - delta)], at(dz=delta))

    def opposite(copy_of, ph):
        ref = copy_of(ph, zz(-6 * way))
        sems = (azs, azr) if copy_of is ref_a else (bzs, bzr)
        return rcopy(ref, ref, sems[0].at[ph], sems[1].at[ph, place(8)], at(dz=2 * way))

    def ref_a(ph, block):
        return G[ph].at[c, block, :, part_a(ph)]

    def ref_b(ph, block):
        return G[ph].at[c, block, x, part_b(ph)]

    def late(d):
        return abs(d) in (5, 7, 8)

    def b_x(ph, d, k):
        ref = ref_b(ph, zz(d))
        kind = 1 if late(d) else (c if k == 0 else 1 - c)
        return rcopy(ref, ref, bxs.at[ph], bxr.at[ph, place(d), kind], at(dx=XD[k]))

    def b_x_on(ph, d):
        ref = G[ph].at[c, zz(d), lax.rem(x - way + X, X), part_b(ph)]
        return rcopy(ref, ref, bxs.at[ph], bxr.at[ph, place(d), 1], at(dx=way))

    def b_x_in(ph, d, kind, count):
        ref = G[ph].at[c, zz(d), pl.ds(0, count), part_b(ph)]
        return rcopy(ref, ref, bxs.at[ph], bxr.at[ph, place(d), kind], sibling)

    def to_sibling(ph, d):
        ref = G[ph].at[c, zz(d)]
        return rcopy(ref, ref, ss.at[ph], sr.at[ph, place(d)], sibling)

    def onward(ph, d, copy, ref_of):
        if d == 0:
            for delta in (3, -3, 1, -1):
                copy(ph, 0, delta).start()
        if abs(d) == 3:
            for delta in (-d, -d // 3, d // 3):
                copy(ph, d, delta).start()
        if abs(d) == 6:
            for delta in (-d // 6, d // 6):
                copy(ph, d, delta).start()

    def A(ph, *ds):
        for d in ds:
            ref = ref_a(ph, zz(d))
            rcopy(ref, ref, azs.at[ph], azr.at[ph, place(d)], sibling).wait_recv()
            onward(ph, d, a_z, ref_a)
        if 6 in ds:
            opposite(ref_a, ph).start()

    def B(ph, *ds):
        for d in ds:
            ref = ref_b(ph, zz(d))
            rcopy(ref, ref, bzs.at[ph], bzr.at[ph, place(d)], sibling).wait_recv()
            onward(ph, d, b_z, ref_b)
        if 6 in ds:
            opposite(ref_b, ph).start()
        for d in ds:
            for k in range(3 if late(d) else 2):
                b_x(ph, d, k).start()

    def F(ph, *ds):
        for d in ds:
            b_x_in(ph, d, 0, 1).wait_recv()
            b_x_on(ph, d).start()

    def S(ph, *ds):
        for d in ds:
            b_x_in(ph, d, 1, 3 if late(d) else 2).wait_recv()
            to_sibling(ph, d).start()

    def AX(ph):
        a_x_in(ph).wait_recv()
        onward(ph, 0, a_z, ref_a)

    def w_y(k):
        dev = at(dy=XD[k])
        return rcopy(
            w_out.at[pl.ds(320 * c, 320), pl.ds(pl.multiple_of(640 * dev[0], 128), 640)],
            wo.at[y, pl.ds(320 * c, 320)], ws.at[k], wr.at[k], dev,
        )

    def w_s(k):
        ref = wo.at[lax.rem(y - XD[k] + Y, Y), pl.ds(320 * c, 320)]
        return rcopy(ref, ref, vs.at[k], vr.at[k], sibling)

    def w_own():
        return pltpu.make_async_copy(
            w_out.at[:, pl.ds(pl.multiple_of(640 * y, 128), 640)], wo.at[y], wl
        )

    def begin(ph):
        onward(ph, 0, b_z, ref_b)
        for k in range(2):
            b_x(ph, 0, k).start()

    for k in range(3):
        a_x(0, k).start()
    begin(0)
    for k in range(3):
        a_x(1, k).start()
    for k in range(3):
        w_y(k).start()
    w_own().start()

    PB[...] = jnp.zeros_like(PB)
    acc[...] = jnp.zeros_like(acc)
    row = lax.broadcasted_iota(jnp.int32, (80, 256), 0)
    lane = lax.broadcasted_iota(jnp.int32, (80, 256), 1)
    base = (lane >> 7) * 40 + ((lane >> 6) & 1) * 20
    r16 = lane & 15
    for xx in range(X):
        here = ((lane >> 4) & 3) == xx
        PB[0, xx, 176:256] = jnp.where(here & (row == base + r16), 1.0, 0.0).astype(BF)
        PB[1, xx, 176:256] = jnp.where(here & (row == base + 16 + (r16 & 3)), 1.0, 0.0).astype(BF)

    fetch.wait()
    lane_j = (lax.broadcasted_iota(jnp.int32, (SPAN, E), 1) & 15) >> 2

    def arrange(m, _):
        window = jnp.minimum(lax.div(80 * m, 128), 3)
        off = pl.multiple_of(176 - (80 * m - 128 * window), 16)
        lhs = jnp.concatenate(
            [tokens[:, pl.ds(pl.multiple_of(640 * xx + 128 * window, 128), 256)] for xx in range(X)], axis=1
        )
        first = dot(lhs, jnp.concatenate([PB[0, xx, pl.ds(off, 256)] for xx in range(X)], axis=0)).astype(BF)
        rest = dot(lhs, jnp.concatenate([PB[1, xx, pl.ds(off, 256)] for xx in range(X)], axis=0))
        for half in range(2):
            T1[2 * m + half] = first[:, half * E:(half + 1) * E]
            part = rest[:, half * E:(half + 1) * E]
            for j in range(4):
                T2[j, 2 * m + half] = jnp.where(lane_j == j, part, 0.0).astype(BF)
        return 0

    lax.fori_loop(0, Z // 2, arrange, 0, unroll=2)

    def M(ph, *ds):
        at_z = [zz(d) for d in ds]
        for d in ds:
            to_sibling(ph, d).wait_recv()

        def column(t):
            return jnp.concatenate([G[ph][:, b, :, t].reshape(E, E) for b in at_z], axis=0)

        def rows(j):
            return jnp.concatenate([T1[b] for b in at_z] + [T2[j, b] for b in at_z], axis=1)

        for i in range(WIDE[ph]):
            u, j, t = i // 4, i % 4, FIRST[ph] + i
            if u == 0 and i + 4 < min(WIDE[ph], 8):
                top = jnp.concatenate([column(i), column(i + 4)], axis=1)
                low = jnp.concatenate([column(WIDE[ph]), column(WIDE[ph] + 1)], axis=1)
                both = dot(rows(j), jnp.concatenate([top, low], axis=0))
                acc[t] += both[:, :E]
                acc[t + 4] += both[:, E:]
            elif u != 1:
                acc[t] += dot(rows(j), jnp.concatenate([column(i), column(WIDE[ph] + u)], axis=0))

    AX(0)
    B(0, 1, -1)
    B(0, 3, -3)
    F(0, 0)
    A(0, 1, -1)
    F(0, 1, -1)
    A(0, 3, -3)
    F(0, 3, -3)
    S(0, 0, 1, -1)
    B(0, 6, -6)
    B(0, 2, -2, 4, -4)
    S(0, 3, -3)
    M(0, 1, -1, 3, -3)
    A(0, 6, -6)
    F(0, 6, -6)
    F(0, 2, -2, 4, -4)
    A(0, 2, -2, 4, -4)
    B(0, 5, -5, 7, -7, 8)
    S(0, 2, -2, 4, -4)
    M(0, 2, -2, 4, -4)
    S(0, 6, -6)
    A(0, 5, -5, 7, -7, 8)
    begin(1)
    AX(1)
    M(0, 0, 6, -6)
    S(0, 5, -5)
    S(0, 7, -7, 8)
    M(0, 5, -5, 7, -7, 8)

    def tile(t):
        return acc[t]

    def silu(v):
        return v / (1.0 + jnp.exp(-v))

    for h in range(HEADS):
        kvq[h] = silu(tile(h)).astype(BF)
        kvq[HEADS + h] = tile(HEADS + h).astype(BF)
        s = lax.dot_general(kvq[h], kvq[HEADS + h], (((0,), (0,)), ((), ())), preferred_element_type=F32)
        state[pl.ds(8 * h, 8)] = s.astype(BF).reshape(8, 16, E)
    pair1 = rcopy(state, sib_state, ps, pr, sibling)
    pair1.start()
    B(1, 1, -1, 3, -3)
    pair1.wait_recv()
    mine = pl.ds(20 * c, 20)
    chip_sum[...] = (state[mine].astype(F32) + sib_state[mine].astype(F32)).astype(BF)

    def owner_z(i):
        return (i * Z) // OWNERS

    def z1(i):
        dst = owner_z(i)
        return rcopy(
            chip_sum.at[pl.ds(SHARE * i, SHARE)], zin.at[z], z1s.at[i], z1r.at[z],
            (y, (x * Z + dst) * 2 + c),
        )

    my_i = lax.div(z * OWNERS + Z - 1, Z)
    is_owner = lax.div(my_i * Z, OWNERS) == z
    for i in range(OWNERS):
        @pl.when(z != owner_z(i))
        def _():
            z1(i).start()

        @pl.when(z == owner_z(i))
        def _():
            zin[z] = chip_sum[pl.ds(SHARE * i, SHARE)]

    F(1, 0)
    A(1, 1, -1, 3, -3)
    F(1, 1, -1, 3, -3)
    B(1, 6, -6, 2, -2, 4, -4)
    S(1, 0, 1, -1, 3, -3)
    M(1, 1, -1, 3, -3)

    def x_copy(k):
        return rcopy(xout, xin.at[x], xs.at[k], xr.at[k], at(dx=XD[k]))

    def z1_in(src):
        return rcopy(chip_sum.at[pl.ds(0, SHARE)], zin.at[src], z1s.at[0], z1r.at[src], sibling)

    def z2(dst):
        return rcopy(
            pout.at[dst], pin.at[pl.ds(SHARE * my_i, SHARE)], z2s.at[dst], z2r.at[my_i],
            (y, (x * Z + dst) * 2 + c),
        )

    def z2_in(i):
        return rcopy(pout.at[0], pin.at[pl.ds(SHARE * i, SHARE)], z2s.at[0], z2r.at[i], sibling)

    @pl.when(is_owner)
    def _():
        for src in range(Z):
            @pl.when(src != z)
            def _():
                z1_in(src).wait_recv()
        total = jnp.zeros((SHARE, 16, E), F32)
        for src in range(Z):
            total = total + zin[src].astype(F32)
        xout[...] = total
        for k in range(3):
            x_copy(k).start()

    F(1, 6, -6, 2, -2, 4, -4)
    A(1, 6, -6, 2, -2, 4, -4)
    B(1, 5, -5, 7, -7, 8)
    S(1, 2, -2, 4, -4)

    @pl.when(is_owner)
    def _():
        for k in range(3):
            x_copy(k).wait_recv()
        running = jnp.zeros((SHARE, 16, E), F32)
        for src in range(X):
            running = running + jnp.where((src < x), xin[src], 0.0)
        for dst in range(Z):
            pout[dst] = running.astype(BF)
            running = running + zin[dst].astype(F32)

            @pl.when(dst != z)
            def _():
                z2(dst).start()
        pin[pl.ds(SHARE * my_i, SHARE)] = pout[z]

    M(1, 2, -2, 4, -4)
    S(1, 6, -6)
    A(1, 5, -5, 7, -7, 8)
    M(1, 0, 6, -6)
    S(1, 5, -5, 7, -7, 8)
    M(1, 5, -5, 7, -7, 8)
    for k in range(3):
        w_y(k).wait_recv()
        w_s(k).start()
    w_own().wait()
    for h in range(HEADS):
        kvq[2 * HEADS + h] = silu(tile(2 * HEADS + h)).astype(BF)
    causal = lax.broadcasted_iota(jnp.int32, (SPAN, SPAN), 0) >= lax.broadcasted_iota(jnp.int32, (SPAN, SPAN), 1)
    for h in range(HEADS):
        q, k, v = kvq[2 * HEADS + h], kvq[h], kvq[HEADS + h]
        scores = lax.dot_general(q, k, (((1,), (1,)), ((), ())), preferred_element_type=F32)
        local[h] = dot(jnp.where(causal, scores, 0.0).astype(BF), v)

    for i in range(OWNERS):
        @pl.when(z != owner_z(i))
        def _():
            z2_in(i).wait_recv()
    pair2 = rcopy(pin, pfull.at[pl.ds(20 * c, 20)], qs, qr, sibling)
    pair2.start()
    pfull[mine] = pin[...]
    pair2.wait_recv()

    def a_y(k, h):
        ref = att.at[y, h]
        return rcopy(ref, ref, ats.at[k], atr.at[c if k == 0 else 1 - c, h], at(dy=XD[k]))

    def a_y_on(h):
        ref = att.at[lax.rem(y - way + Y, Y), h]
        return rcopy(ref, ref, ats.at[2], atr.at[2, h], at(dy=way))

    def a_y_in(kind, h):
        return rcopy(att.at[y, h], att.at[y, h], ats.at[0], atr.at[kind, h], sibling)

    for h in range(HEADS):
        before = pfull[pl.ds(8 * h, 8)].reshape(E, E).astype(F32)
        first = sib_state[pl.ds(8 * h, 8)].reshape(E, E).astype(F32)
        prefix = jnp.where(c == 1, before + first, before).astype(BF)
        combined = dot(kvq[2 * HEADS + h], prefix) + local[h]
        scale = lax.rsqrt(jnp.mean(combined * combined, axis=-1, keepdims=True) + 1e-05)
        att[y, h] = (combined * scale * gain[h:h + 1].astype(F32)).astype(BF)
        for k in range(2):
            a_y(k, h).start()

    def project(section):
        lhs = jnp.concatenate([att[section, h] for h in range(HEADS)], axis=1)
        return dot(lhs, wo[section])

    for k in range(3):
        w_s(k).wait_recv()
    total = tokens[:, pl.ds(pl.multiple_of(640 * y, 128), 640)].astype(F32) + project(y)
    for h in range(HEADS):
        a_y_in(0, h).wait_recv()
        a_y_on(h).start()
    total = total + project(lax.rem(y - way + Y, Y))

    for k in range(3):
        w_y(k).wait_send()
        w_s(k).wait_send()

    def sent(ref, sem):
        rcopy(ref, ref, sem, sem, sibling).wait_send()

    for ph in range(2):
        sent(G[ph].at[c, z, pl.ds(0, 3), part_a(ph)], axs.at[ph])
        sent(G[ph].at[c, pl.ds(0, Z - 1), :, part_a(ph)], azs.at[ph])
        sent(G[ph].at[c, pl.ds(0, Z - 1), x, part_b(ph)], bzs.at[ph])
        sent(G[ph].at[c, :, pl.ds(0, 3), part_b(ph)], bxs.at[ph])
        sent(G[ph].at[c], ss.at[ph])
    pair1.wait_send()
    pair2.wait_send()
    for i in range(OWNERS):
        @pl.when(z != owner_z(i))
        def _():
            z1(i).wait_send()

    @pl.when(is_owner)
    def _():
        for k in range(3):
            x_copy(k).wait_send()
        for dst in range(Z):
            @pl.when(dst != z)
            def _():
                z2(dst).wait_send()

    for kind, section in ((1, y + way), (2, y + 2)):
        for h in range(HEADS):
            a_y_in(kind, h).wait_recv()
        total = total + project(lax.rem(section + Y, Y))
    out[...] = total.astype(BF)
    for k in range(3):
        sent(att.at[0], ats.at[k])


def on_device(tokens, w_query, w_key, w_value, gain, w_out):
    vmem = pl.BlockSpec(memory_space=pltpu.VMEM)
    hbm = pl.BlockSpec(memory_space=pl.ANY)
    dma = pltpu.SemaphoreType.DMA
    return pl.pallas_call(
        kernel,
        name="layer",
        out_shape=jax.ShapeDtypeStruct((SPAN, 640), BF),
        in_specs=[hbm, vmem, vmem, vmem, vmem, hbm],
        out_specs=vmem,
        scratch_shapes=[
            pltpu.VMEM((SPAN, 2560), BF),
            pltpu.VMEM((2, Z, X, TILES[0], 16, E), BF),
            pltpu.VMEM((2, Z, X, TILES[1], 16, E), BF),
            pltpu.VMEM((Z, SPAN, E), BF),
            pltpu.VMEM((4, Z, SPAN, E), BF),
            pltpu.VMEM((2, X, 432, 256), BF),
            pltpu.VMEM((COLS, SPAN, E), F32),
            pltpu.VMEM((Y, 640, 640), BF),
            pltpu.VMEM((COLS, SPAN, E), BF),
            pltpu.VMEM((HEADS, SPAN, E), F32),
            pltpu.VMEM((Y, HEADS, SPAN, E), BF),
            pltpu.VMEM((40, 16, E), BF),
            pltpu.VMEM((40, 16, E), BF),
            pltpu.VMEM((20, 16, E), BF),
            pltpu.VMEM((Z, SHARE, 16, E), BF),
            pltpu.VMEM((SHARE, 16, E), F32),
            pltpu.VMEM((X, SHARE, 16, E), F32),
            pltpu.VMEM((Z, SHARE, 16, E), BF),
            pltpu.VMEM((20, 16, E), BF),
            pltpu.VMEM((40, 16, E), BF),
            dma((2,)), dma((2,)),
            dma((2,)), dma((2, Z)),
            dma((2,)), dma((2, Z)),
            dma((2,)), dma((2, Z, 2)),
            dma((2,)), dma((2, Z)),
            dma((3,)), dma((3,)), dma((3,)), dma((3,)), dma(()),
            dma(()), dma(()),
            dma((OWNERS,)), dma((Z,)),
            dma((3,)), dma((3,)),
            dma((Z,)), dma((OWNERS,)),
            dma(()), dma(()),
            dma((3,)), dma((3, HEADS)), dma(()),
        ],
        compiler_params=pltpu.CompilerParams(
            collective_id=1, has_side_effects=True, vmem_limit_bytes=56 << 20
        ),
    )(tokens, w_query, w_key, w_value, gain.reshape(HEADS, E), w_out)


def solution(mesh):
    placed = (
        P("seq", None),
        P("seq", "section"),
        P("seq", "section"),
        P("seq", "section"),
        P("section"),
        P("section", None),
    )
    return jax.shard_map(
        on_device, mesh=mesh, in_specs=placed, out_specs=P("seq", "section"), check_vma=False
    )
```

```python
import jax
import jax.numpy as jnp
from jax import lax
from jax.experimental import pallas as pl
from jax.experimental.pallas import tpu as pltpu
from jax.sharding import PartitionSpec as P

E = 128
X, Z, Y = 4, 16, 4
ROWS = 20
HEADS = 5
COLS = 3 * HEADS
FIRST = (0, 2 * HEADS)
WIDE = (2 * HEADS, HEADS)
TILES = (13, 7)
CUT = (2, 2)
SPAN = 256
OWNERS, SHARE = 10, 2
MESH = pl.DeviceIdType.MESH
BF = jnp.bfloat16
F32 = jnp.float32


def dot(a, b):
    return jnp.dot(a, b, preferred_element_type=F32)


def kernel(
    tokens_hbm, wq, wk, wv, gain, w_out, out, tokens,
    G0, G1, T1, T2, PB, acc, wo, kvq, local, att,
    state, sib_state, chip_sum, zin, xout, xin, pout, pfull,
    axs, axr, azs, azr, bzs, bzr, bxs, bxr, ss, sr,
    ws, wr, vs, vr, wl, ps, pr, z1s, z1r, xs, xr, z2s, z2r, qs, qr, ats, atr, tl,
):
    seq = lax.axis_index("seq")
    y = lax.axis_index("section")
    c = lax.rem(seq, 2)
    z = lax.rem(lax.div(seq, 2), Z)
    x = lax.div(seq, 2 * Z)

    def at(dx=0, dy=0, dz=0, core=None):
        core = c if core is None else core
        nx, ny, nz = lax.rem(x + dx + X, X), lax.rem(y + dy + Y, Y), lax.rem(z + dz + Z, Z)
        return (ny, (nx * Z + nz) * 2 + core)

    def zz(d):
        return lax.rem(z + d + Z, Z)

    def rcopy(src, dst, ssem, rsem, dev):
        return pltpu.make_async_remote_copy(
            src_ref=src, dst_ref=dst, send_sem=ssem, recv_sem=rsem,
            device_id=dev, device_id_type=MESH,
        )

    sibling = at(core=1 - c)

    way = 1 - 2 * c
    G = (G0, G1)

    barrier = pltpu.get_barrier_semaphore()
    greeted = [at(dz=d) for d in (1, -1, 2, -2, 3, -3)] + [at(dx=1), at(dx=-1), at(dx=2), sibling]
    greeted += [at(dy=1), at(dy=-1), at(dy=2)]
    for dev in greeted:
        pl.semaphore_signal(barrier, inc=1, device_id=dev, device_id_type=MESH)
    fetch = pltpu.make_async_copy(tokens_hbm, tokens, tl)
    fetch.start()

    weights = (wk, wv, wq)
    for ph in range(2):
        for i in range(WIDE[ph]):
            t = FIRST[ph] + i
            G[ph][c, z, x, i] = weights[t // HEADS][0:16, pl.ds((t % HEADS) * E, E)]
        for u in range(TILES[ph] - WIDE[ph]):
            parts = []
            for i in range(4 * u, 4 * u + 4):
                t = FIRST[ph] + i
                if i < WIDE[ph]:
                    parts.append(weights[t // HEADS][16:20, pl.ds((t % HEADS) * E, E)].astype(F32))
                else:
                    parts.append(jnp.zeros((4, E), F32))
            G[ph][c, z, x, WIDE[ph] + u] = jnp.concatenate(parts, axis=0).astype(BF)

    pl.semaphore_wait(barrier, len(greeted))

    XD = (1, -1, 2)

    def place(d):
        return (d + 7) % Z

    def part_a(ph):
        return pl.ds(0, CUT[ph])

    def part_b(ph):
        return pl.ds(CUT[ph], TILES[ph] - CUT[ph])

    def a_x(ph, k):
        ref = G[ph].at[c, z, x, part_a(ph)]
        return rcopy(ref, ref, axs.at[ph], axr.at[ph], at(dx=XD[k]))

    def a_x_in(ph):
        ref = G[ph].at[c, z, pl.ds(0, 3), part_a(ph)]
        return rcopy(ref, ref, axs.at[ph], axr.at[ph], sibling)

    def a_z(ph, d, delta):
        ref = G[ph].at[c, zz(d), :, part_a(ph)]
        return rcopy(ref, ref, azs.at[ph], azr.at[ph, place(d - delta)], at(dz=delta))

    def b_z(ph, d, delta):
        ref = G[ph].at[c, zz(d), x, part_b(ph)]
        return rcopy(ref, ref, bzs.at[ph], bzr.at[ph, place(d - delta)], at(dz=delta))

    def opposite(copy_of, ph):
        ref = copy_of(ph, zz(-6 * way))
        sems = (azs, azr) if copy_of is ref_a else (bzs, bzr)
        return rcopy(ref, ref, sems[0].at[ph], sems[1].at[ph, place(8)], at(dz=2 * way))

    def ref_a(ph, block):
        return G[ph].at[c, block, :, part_a(ph)]

    def ref_b(ph, block):
        return G[ph].at[c, block, x, part_b(ph)]

    def late(d):
        return abs(d) in (5, 7, 8)

    def b_x(ph, d, k):
        ref = ref_b(ph, zz(d))
        kind = 1 if late(d) else (c if k == 0 else 1 - c)
        return rcopy(ref, ref, bxs.at[ph], bxr.at[ph, place(d), kind], at(dx=XD[k]))

    def b_x_on(ph, d):
        ref = G[ph].at[c, zz(d), lax.rem(x - way + X, X), part_b(ph)]
        return rcopy(ref, ref, bxs.at[ph], bxr.at[ph, place(d), 1], at(dx=way))

    def b_x_in(ph, d, kind, count):
        ref = G[ph].at[c, zz(d), pl.ds(0, count), part_b(ph)]
        return rcopy(ref, ref, bxs.at[ph], bxr.at[ph, place(d), kind], sibling)

    def to_sibling(ph, d):
        ref = G[ph].at[c, zz(d)]
        return rcopy(ref, ref, ss.at[ph], sr.at[ph, place(d)], sibling)

    def onward(ph, d, copy):
        jumps = {0: (3, -3, 1, -1), 3: (-3, -1, 1), 6: (-1, 1)}.get(abs(d), ())
        for jump in jumps:
            copy(ph, d, jump if d >= 0 else -jump).start()

    def A(ph, *ds):
        for d in ds:
            ref = ref_a(ph, zz(d))
            rcopy(ref, ref, azs.at[ph], azr.at[ph, place(d)], sibling).wait_recv()
            onward(ph, d, a_z)
        if 6 in ds:
            opposite(ref_a, ph).start()

    def BZ(ph, *ds):
        for d in ds:
            ref = ref_b(ph, zz(d))
            rcopy(ref, ref, bzs.at[ph], bzr.at[ph, place(d)], sibling).wait_recv()
            onward(ph, d, b_z)
        if 6 in ds:
            opposite(ref_b, ph).start()

    def BX(ph, *ds):
        for d in ds:
            for k in range(3 if late(d) else 2):
                b_x(ph, d, k).start()

    def B(ph, *ds):
        BZ(ph, *ds)
        BX(ph, *ds)

    def F(ph, *ds):
        for d in ds:
            b_x_in(ph, d, 0, 1).wait_recv()
            b_x_on(ph, d).start()

    def S(ph, *ds):
        for d in ds:
            b_x_in(ph, d, 1, 3 if late(d) else 2).wait_recv()
            to_sibling(ph, d).start()

    def AX(ph):
        a_x_in(ph).wait_recv()
        onward(ph, 0, a_z)

    def w_y(k):
        dev = at(dy=XD[k])
        return rcopy(
            w_out.at[pl.ds(320 * c, 320), pl.ds(pl.multiple_of(640 * dev[0], 128), 640)],
            wo.at[y, pl.ds(320 * c, 320)], ws.at[k], wr.at[k], dev,
        )

    def w_s(k):
        ref = wo.at[lax.rem(y - XD[k] + Y, Y), pl.ds(320 * c, 320)]
        return rcopy(ref, ref, vs.at[k], vr.at[k], sibling)

    def w_own():
        return pltpu.make_async_copy(
            w_out.at[:, pl.ds(pl.multiple_of(640 * y, 128), 640)], wo.at[y], wl
        )

    def begin(ph):
        onward(ph, 0, b_z)
        for k in range(2):
            b_x(ph, 0, k).start()

    for k in range(3):
        a_x(0, k).start()
    begin(0)
    for k in range(3):
        a_x(1, k).start()
    for k in range(3):
        w_y(k).start()
    w_own().start()

    PB[...] = jnp.zeros_like(PB)
    acc[...] = jnp.zeros_like(acc)
    row = lax.broadcasted_iota(jnp.int32, (80, 256), 0)
    lane = lax.broadcasted_iota(jnp.int32, (80, 256), 1)
    base = (lane >> 7) * 40 + ((lane >> 6) & 1) * 20
    r16 = lane & 15
    for xx in range(X):
        here = ((lane >> 4) & 3) == xx
        PB[0, xx, 176:256] = jnp.where(here & (row == base + r16), 1.0, 0.0).astype(BF)
        PB[1, xx, 176:256] = jnp.where(here & (row == base + 16 + (r16 & 3)), 1.0, 0.0).astype(BF)

    fetch.wait()
    lane_j = (lax.broadcasted_iota(jnp.int32, (SPAN, E), 1) & 15) >> 2

    def arrange(m, _):
        window = jnp.minimum(lax.div(80 * m, 128), 3)
        off = pl.multiple_of(176 - (80 * m - 128 * window), 16)
        lhs = jnp.concatenate(
            [tokens[:, pl.ds(pl.multiple_of(640 * xx + 128 * window, 128), 256)] for xx in range(X)], axis=1
        )
        first = dot(lhs, jnp.concatenate([PB[0, xx, pl.ds(off, 256)] for xx in range(X)], axis=0)).astype(BF)
        rest = dot(lhs, jnp.concatenate([PB[1, xx, pl.ds(off, 256)] for xx in range(X)], axis=0))
        for half in range(2):
            T1[2 * m + half] = first[:, half * E:(half + 1) * E]
            part = rest[:, half * E:(half + 1) * E]
            for j in range(4):
                T2[j, 2 * m + half] = jnp.where(lane_j == j, part, 0.0).astype(BF)
        return 0

    lax.fori_loop(0, Z // 2, arrange, 0, unroll=2)

    def M(ph, *ds):
        at_z = [zz(d) for d in ds]
        for d in ds:
            to_sibling(ph, d).wait_recv()

        def column(t):
            return jnp.concatenate([G[ph][:, b, :, t].reshape(E, E) for b in at_z], axis=0)

        def rows(j):
            return jnp.concatenate([T1[b] for b in at_z] + [T2[j, b] for b in at_z], axis=1)

        for i in range(WIDE[ph]):
            u, j, t = i // 4, i % 4, FIRST[ph] + i
            if u == 0 and i + 4 < min(WIDE[ph], 8):
                top = jnp.concatenate([column(i), column(i + 4)], axis=1)
                low = jnp.concatenate([column(WIDE[ph]), column(WIDE[ph] + 1)], axis=1)
                both = dot(rows(j), jnp.concatenate([top, low], axis=0))
                acc[t] += both[:, :E]
                acc[t + 4] += both[:, E:]
            elif u != 1:
                acc[t] += dot(rows(j), jnp.concatenate([column(i), column(WIDE[ph] + u)], axis=0))

    AX(0)
    B(0, 1, -1)
    B(0, 3, -3)
    F(0, 0)
    A(0, 1, -1)
    F(0, 1, -1)
    A(0, 3, -3)
    F(0, 3, -3)
    S(0, 0, 1, -1)
    B(0, 6, -6)
    B(0, 2, -2, 4, -4)
    S(0, 3, -3)
    M(0, 1, -1, 3, -3)
    A(0, 6, -6)
    F(0, 6, -6)
    F(0, 2, -2, 4, -4)
    A(0, 2, -2, 4, -4)
    B(0, 5, -5, 7, -7, 8)
    onward(1, 0, b_z)
    AX(1)
    S(0, 2, -2, 4, -4)
    BZ(1, 1, -1)
    BZ(1, 3, -3)
    M(0, 2, -2, 4, -4)
    S(0, 6, -6)
    A(0, 5, -5, 7, -7, 8)
    A(1, 1, -1)
    A(1, 3, -3)
    M(0, 0, 6, -6)
    S(0, 5, -5)
    BZ(1, 6, -6)
    BZ(1, 2, -2, 4, -4)
    S(0, 7, -7, 8)
    BX(1, 0, 1, -1, 3, -3)
    M(0, 5, -5, 7, -7, 8)

    def tile(t):
        return acc[t]

    def silu(v):
        return v / (1.0 + jnp.exp(-v))

    for h in range(HEADS):
        kvq[h] = silu(tile(h)).astype(BF)
        kvq[HEADS + h] = tile(HEADS + h).astype(BF)
        s = lax.dot_general(kvq[h], kvq[HEADS + h], (((0,), (0,)), ((), ())), preferred_element_type=F32)
        state[pl.ds(8 * h, 8)] = s.astype(BF).reshape(8, 16, E)
    pair1 = rcopy(state, sib_state, ps, pr, sibling)
    pair1.start()
    BX(1, 6, -6, 2, -2, 4, -4)
    A(1, 6, -6)
    A(1, 2, -2, 4, -4)
    pair1.wait_recv()
    mine = pl.ds(20 * c, 20)
    chip_sum[...] = (state[mine].astype(F32) + sib_state[mine].astype(F32)).astype(BF)

    def owner_z(i):
        return (i * Z) // OWNERS

    def z1(i):
        dst = owner_z(i)
        return rcopy(
            chip_sum.at[pl.ds(SHARE * i, SHARE)], zin.at[z], z1s, z1r.at[z],
            (y, (x * Z + dst) * 2 + c),
        )

    my_i = lax.div(z * OWNERS + Z - 1, Z)
    is_owner = lax.div(my_i * Z, OWNERS) == z
    for i in range(OWNERS):
        @pl.when(z != owner_z(i))
        def _():
            z1(i).start()

        @pl.when(z == owner_z(i))
        def _():
            zin[z] = chip_sum[pl.ds(SHARE * i, SHARE)]

    BZ(1, 5, -5, 7, -7, 8)
    BX(1, 5, -5, 7, -7, 8)
    F(1, 0, 1, -1, 3, -3)

    def x_copy(k):
        return rcopy(xout, xin.at[x], xs.at[k], xr.at[k], at(dx=XD[k]))

    def z1_in(src):
        return rcopy(chip_sum.at[pl.ds(0, SHARE)], zin.at[src], z1s, z1r.at[src], sibling)

    def z2(dst):
        return rcopy(
            pout.at[dst], pfull.at[pl.ds(20 * c + SHARE * my_i, SHARE)], z2s, z2r.at[my_i],
            (y, (x * Z + dst) * 2 + c),
        )

    def z2_in(i):
        return rcopy(pout.at[0], pfull.at[pl.ds(20 * c + SHARE * i, SHARE)], z2s, z2r.at[i], sibling)

    @pl.when(is_owner)
    def _():
        for src in range(Z):
            @pl.when(src != z)
            def _():
                z1_in(src).wait_recv()
        total = jnp.zeros((SHARE, 16, E), F32)
        for src in range(Z):
            total = total + zin[src].astype(F32)
        xout[...] = total
        for k in range(3):
            x_copy(k).start()

    S(1, 0, 1, -1, 3, -3)
    F(1, 6, -6, 2, -2, 4, -4)
    M(1, 1, -1, 3, -3)

    @pl.when(is_owner)
    def _():
        for k in range(3):
            x_copy(k).wait_recv()
        running = jnp.zeros((SHARE, 16, E), F32)
        for src in range(X):
            running = running + jnp.where((src < x), xin[src], 0.0)
        for dst in range(Z):
            pout[dst] = running.astype(BF)
            running = running + zin[dst].astype(F32)

            @pl.when(dst != z)
            def _():
                z2(dst).start()
        pfull[pl.ds(20 * c + SHARE * my_i, SHARE)] = pout[z]

    S(1, 2, -2, 4, -4)
    S(1, 6, -6)
    A(1, 5, -5, 7, -7, 8)
    S(1, 5, -5, 7, -7, 8)
    M(1, 2, -2, 4, -4)
    M(1, 0, 6, -6)
    M(1, 5, -5, 7, -7, 8)
    for k in range(3):
        w_y(k).wait_recv()
        w_s(k).start()
    w_own().wait()
    for h in range(HEADS):
        kvq[2 * HEADS + h] = silu(tile(2 * HEADS + h)).astype(BF)
    causal = lax.broadcasted_iota(jnp.int32, (SPAN, SPAN), 0) >= lax.broadcasted_iota(jnp.int32, (SPAN, SPAN), 1)
    for h in range(HEADS):
        q, k, v = kvq[2 * HEADS + h], kvq[h], kvq[HEADS + h]
        scores = lax.dot_general(q, k, (((1,), (1,)), ((), ())), preferred_element_type=F32)
        local[h] = dot(jnp.where(causal, scores, 0.0).astype(BF), v)

    def a_y(k, n, h):
        ref = att.at[y, h]
        return rcopy(ref, ref, ats.at[k], atr.at[c if k == 0 else 1 - c, n], at(dy=XD[k]))

    def a_y_on(n):
        ref = att.at[lax.rem(y - way + Y, Y), nth(n)]
        return rcopy(ref, ref, ats.at[2], atr.at[2, n], at(dy=way))

    def a_y_in(kind, n):
        return rcopy(att.at[y, 0], att.at[y, 0], ats.at[0], atr.at[kind, n], sibling)

    def nth(n):
        return lax.rem(n + 3 * c, HEADS)

    def pair2(n):
        first, size = (4 * c, 8) if n == 0 else ((4 * c + 8, 8) if n == 1 else (16 * (1 - c), 4))
        ref = pfull.at[pl.ds(20 * c + first, size)]
        return rcopy(ref, ref, qs.at[n], qr.at[n], sibling)

    def combine(n):
        h = nth(n)
        before = pfull[pl.ds(8 * h, 8)].reshape(E, E).astype(F32)
        first = sib_state[pl.ds(8 * h, 8)].reshape(E, E).astype(F32)
        prefix = jnp.where(c == 1, before + first, before).astype(BF)
        combined = dot(kvq[2 * HEADS + h], prefix) + local[h]
        scale = lax.rsqrt(jnp.mean(combined * combined, axis=-1, keepdims=True) + 1e-05)
        att[y, h] = (combined * scale * gain[h]).astype(BF)
        for k in range(2):
            a_y(k, n, h).start()

    for n, order in enumerate(((0, 1, 2, 3), (4, 5, 6, 7), (8, 9))):
        for i in order:
            i = lax.rem(i + 2 * c, OWNERS)

            @pl.when(z != lax.div(i * Z, OWNERS))
            def _():
                z2_in(i).wait_recv()
        pair2(n).start()
        if n < 2:
            combine(n)
    for n in range(3):
        pair2(n).wait_recv()
    for n in range(2, HEADS):
        combine(n)

    def project(section):
        lhs = jnp.concatenate([att[section, h] for h in range(HEADS)], axis=1)
        return dot(lhs, wo[section])

    for k in range(3):
        w_s(k).wait_recv()
    total = tokens[:, pl.ds(pl.multiple_of(640 * y, 128), 640)].astype(F32) + project(y)
    for n in range(HEADS):
        a_y_in(0, n).wait_recv()
        a_y_on(n).start()
    total = total + project(lax.rem(y - way + Y, Y))

    for k in range(3):
        w_y(k).wait_send()
        w_s(k).wait_send()

    def sent(ref, sem):
        rcopy(ref, ref, sem, sem, sibling).wait_send()

    for ph in range(2):
        sent(G[ph].at[c, z, pl.ds(0, 3), part_a(ph)], axs.at[ph])
        sent(G[ph].at[c, pl.ds(0, Z - 1), :, part_a(ph)], azs.at[ph])
        sent(G[ph].at[c, pl.ds(0, Z - 1), x, part_b(ph)], bzs.at[ph])
        sent(G[ph].at[c, :, pl.ds(0, 3), part_b(ph)], bxs.at[ph])
        sent(G[ph].at[c], ss.at[ph])
    pair1.wait_send()
    for n in range(3):
        pair2(n).wait_send()
    @pl.when(is_owner)
    def _():
        sent(chip_sum.at[pl.ds(0, SHARE * (OWNERS - 1))], z1s)
        sent(pout.at[pl.ds(0, Z - 1)], z2s)
        for k in range(3):
            x_copy(k).wait_send()

    @pl.when(jnp.logical_not(is_owner))
    def _():
        sent(chip_sum, z1s)

    for kind, section in ((1, y + way), (2, y + 2)):
        for n in range(HEADS):
            a_y_in(kind, n).wait_recv()
        total = total + project(lax.rem(section + Y, Y))
    out[...] = total.astype(BF)
    for k in range(3):
        sent(att.at[0], ats.at[k])


def on_device(tokens, w_query, w_key, w_value, gain, w_out):
    vmem = pl.BlockSpec(memory_space=pltpu.VMEM)
    hbm = pl.BlockSpec(memory_space=pl.ANY)
    dma = pltpu.SemaphoreType.DMA
    return pl.pallas_call(
        kernel,
        name="layer",
        out_shape=jax.ShapeDtypeStruct((SPAN, 640), BF),
        in_specs=[hbm, vmem, vmem, vmem, vmem, hbm],
        out_specs=vmem,
        scratch_shapes=[
            pltpu.VMEM((SPAN, 2560), BF),
            pltpu.VMEM((2, Z, X, TILES[0], 16, E), BF),
            pltpu.VMEM((2, Z, X, TILES[1], 16, E), BF),
            pltpu.VMEM((Z, SPAN, E), BF),
            pltpu.VMEM((4, Z, SPAN, E), BF),
            pltpu.VMEM((2, X, 432, 256), BF),
            pltpu.VMEM((COLS, SPAN, E), F32),
            pltpu.VMEM((Y, 640, 640), BF),
            pltpu.VMEM((COLS, SPAN, E), BF),
            pltpu.VMEM((HEADS, SPAN, E), F32),
            pltpu.VMEM((Y, HEADS, SPAN, E), BF),
            pltpu.VMEM((40, 16, E), BF),
            pltpu.VMEM((40, 16, E), BF),
            pltpu.VMEM((20, 16, E), BF),
            pltpu.VMEM((Z, SHARE, 16, E), BF),
            pltpu.VMEM((SHARE, 16, E), F32),
            pltpu.VMEM((X, SHARE, 16, E), F32),
            pltpu.VMEM((Z, SHARE, 16, E), BF),
            pltpu.VMEM((40, 16, E), BF),
            dma((2,)), dma((2,)),
            dma((2,)), dma((2, Z)),
            dma((2,)), dma((2, Z)),
            dma((2,)), dma((2, Z, 2)),
            dma((2,)), dma((2, Z)),
            dma((3,)), dma((3,)), dma((3,)), dma((3,)), dma(()),
            dma(()), dma(()),
            dma(()), dma((Z,)),
            dma((3,)), dma((3,)),
            dma(()), dma((OWNERS,)),
            dma((3,)), dma((3,)),
            dma((3,)), dma((3, HEADS)), dma(()),
        ],
        compiler_params=pltpu.CompilerParams(
            collective_id=1, has_side_effects=True, vmem_limit_bytes=56 << 20
        ),
    )(tokens, w_query, w_key, w_value, gain.astype(F32).reshape(HEADS, 1, E), w_out)


def solution(mesh):
    placed = (
        P("seq", None),
        P("seq", "section"),
        P("seq", "section"),
        P("seq", "section"),
        P("section"),
        P("section", None),
    )
    return jax.shard_map(
        on_device, mesh=mesh, in_specs=placed, out_specs=P("seq", "section"), check_vma=False
    )
```

```python
import jax
import jax.numpy as jnp
from jax import lax
from jax.experimental import pallas as pl
from jax.experimental.pallas import tpu as pltpu
from jax.sharding import PartitionSpec as P

E = 128
X, Z, Y = 4, 16, 4
ROWS = 20
HEADS = 5
COLS = 3 * HEADS
FIRST = (0, 2 * HEADS)
WIDE = (2 * HEADS, HEADS)
TILES = (13, 7)
CUT = (2, 2)
SPAN = 256
OWNERS, SHARE = 10, 2
MESH = pl.DeviceIdType.MESH
BF = jnp.bfloat16
F32 = jnp.float32


def dot(a, b):
    return jnp.dot(a, b, preferred_element_type=F32)


def kernel(
    tokens_hbm, wq, wk, wv, gain, w_out, out, tokens,
    gain_rows, G0, G1, T1, T2, PB, acc, wo, kvq, local, att,
    state, sib_state, chip_sum, zin, xout, xin, pout, pfull,
    axs, axr, azs, azr, bzs, bzr, bxs, bxr, ss, sr,
    ws, wr, vs, vr, wl, ps, pr, z1s, z1r, xs, xr, z2s, z2r, qs, qr, ats, atr, tl,
):
    seq = lax.axis_index("seq")
    y = lax.axis_index("section")
    c = lax.rem(seq, 2)
    z = lax.rem(lax.div(seq, 2), Z)
    x = lax.div(seq, 2 * Z)

    def at(dx=0, dy=0, dz=0, core=None):
        core = c if core is None else core
        nx, ny, nz = lax.rem(x + dx + X, X), lax.rem(y + dy + Y, Y), lax.rem(z + dz + Z, Z)
        return (ny, (nx * Z + nz) * 2 + core)

    def zz(d):
        return lax.rem(z + d + Z, Z)

    def rcopy(src, dst, ssem, rsem, dev):
        return pltpu.make_async_remote_copy(
            src_ref=src, dst_ref=dst, send_sem=ssem, recv_sem=rsem,
            device_id=dev, device_id_type=MESH,
        )

    sibling = at(core=1 - c)

    way = 1 - 2 * c
    G = (G0, G1)

    barrier = pltpu.get_barrier_semaphore()
    greeted = [at(dz=d) for d in (1, -1, 2, -2, 3, -3)] + [at(dx=1), at(dx=-1), at(dx=2), sibling]
    greeted += [at(dy=1), at(dy=-1), at(dy=2)]
    for dev in greeted:
        pl.semaphore_signal(barrier, inc=1, device_id=dev, device_id_type=MESH)
    fetch = pltpu.make_async_copy(tokens_hbm, tokens, tl)
    fetch.start()

    weights = (wk, wv, wq)
    for ph in range(2):
        for i in range(WIDE[ph]):
            t = FIRST[ph] + i
            G[ph][c, z, x, i] = weights[t // HEADS][0:16, pl.ds((t % HEADS) * E, E)]
        for u in range(TILES[ph] - WIDE[ph]):
            parts = []
            for i in range(4 * u, 4 * u + 4):
                t = FIRST[ph] + i
                if i < WIDE[ph]:
                    parts.append(weights[t // HEADS][16:20, pl.ds((t % HEADS) * E, E)].astype(F32))
                else:
                    parts.append(jnp.zeros((4, E), F32))
            G[ph][c, z, x, WIDE[ph] + u] = jnp.concatenate(parts, axis=0).astype(BF)

    pl.semaphore_wait(barrier, len(greeted))

    XD = (1, -1, 2)

    def place(d):
        return (d + 7) % Z

    def part_a(ph):
        return pl.ds(0, CUT[ph])

    def part_b(ph):
        return pl.ds(CUT[ph], TILES[ph] - CUT[ph])

    def a_x(ph, k):
        ref = G[ph].at[c, z, x, part_a(ph)]
        return rcopy(ref, ref, axs.at[ph], axr.at[ph], at(dx=XD[k]))

    def a_x_in(ph):
        ref = G[ph].at[c, z, pl.ds(0, 3), part_a(ph)]
        return rcopy(ref, ref, axs.at[ph], axr.at[ph], sibling)

    def a_z(ph, d, delta):
        ref = G[ph].at[c, zz(d), :, part_a(ph)]
        return rcopy(ref, ref, azs.at[ph], azr.at[ph, place(d - delta)], at(dz=delta))

    def b_z(ph, d, delta):
        ref = G[ph].at[c, zz(d), x, part_b(ph)]
        return rcopy(ref, ref, bzs.at[ph], bzr.at[ph, place(d - delta)], at(dz=delta))

    def opposite(copy_of, ph):
        ref = copy_of(ph, zz(-6 * way))
        sems = (azs, azr) if copy_of is ref_a else (bzs, bzr)
        return rcopy(ref, ref, sems[0].at[ph], sems[1].at[ph, place(8)], at(dz=2 * way))

    def ref_a(ph, block):
        return G[ph].at[c, block, :, part_a(ph)]

    def ref_b(ph, block):
        return G[ph].at[c, block, x, part_b(ph)]

    def late(d):
        return abs(d) in (5, 7, 8)

    def b_x(ph, d, k):
        ref = ref_b(ph, zz(d))
        kind = 1 if late(d) else (c if k == 0 else 1 - c)
        return rcopy(ref, ref, bxs.at[ph], bxr.at[ph, place(d), kind], at(dx=XD[k]))

    def b_x_on(ph, d):
        ref = G[ph].at[c, zz(d), lax.rem(x - way + X, X), part_b(ph)]
        return rcopy(ref, ref, bxs.at[ph], bxr.at[ph, place(d), 1], at(dx=way))

    def b_x_in(ph, d, kind, count):
        ref = G[ph].at[c, zz(d), pl.ds(0, count), part_b(ph)]
        return rcopy(ref, ref, bxs.at[ph], bxr.at[ph, place(d), kind], sibling)

    def to_sibling(ph, d):
        ref = G[ph].at[c, zz(d)]
        return rcopy(ref, ref, ss.at[ph], sr.at[ph, place(d)], sibling)

    def onward(ph, d, copy):
        jumps = {0: (3, -3, 1, -1), 3: (-3, -1, 1), 6: (-1, 1)}.get(abs(d), ())
        for jump in jumps:
            copy(ph, d, jump if d >= 0 else -jump).start()

    def A(ph, *ds):
        for d in ds:
            ref = ref_a(ph, zz(d))
            rcopy(ref, ref, azs.at[ph], azr.at[ph, place(d)], sibling).wait_recv()
            onward(ph, d, a_z)
        if 6 in ds:
            opposite(ref_a, ph).start()

    def BZ(ph, *ds):
        for d in ds:
            ref = ref_b(ph, zz(d))
            rcopy(ref, ref, bzs.at[ph], bzr.at[ph, place(d)], sibling).wait_recv()
            onward(ph, d, b_z)
        if 6 in ds:
            opposite(ref_b, ph).start()

    def BX(ph, *ds):
        for d in ds:
            for k in range(3 if late(d) else 2):
                b_x(ph, d, k).start()

    def B(ph, *ds):
        BZ(ph, *ds)
        BX(ph, *ds)

    def F(ph, *ds):
        for d in ds:
            b_x_in(ph, d, 0, 1).wait_recv()
            b_x_on(ph, d).start()

    def S(ph, *ds):
        for d in ds:
            b_x_in(ph, d, 1, 3 if late(d) else 2).wait_recv()
            to_sibling(ph, d).start()

    def AX(ph):
        a_x_in(ph).wait_recv()
        onward(ph, 0, a_z)

    def w_y(k):
        dev = at(dy=XD[k])
        return rcopy(
            w_out.at[pl.ds(320 * c, 320), pl.ds(pl.multiple_of(640 * dev[0], 128), 640)],
            wo.at[y, pl.ds(320 * c, 320)], ws.at[k], wr.at[k], dev,
        )

    def w_s(k):
        ref = wo.at[lax.rem(y - XD[k] + Y, Y), pl.ds(320 * c, 320)]
        return rcopy(ref, ref, vs.at[k], vr.at[k], sibling)

    def w_own():
        return pltpu.make_async_copy(
            w_out.at[:, pl.ds(pl.multiple_of(640 * y, 128), 640)], wo.at[y], wl
        )

    def begin(ph):
        onward(ph, 0, b_z)
        for k in range(2):
            b_x(ph, 0, k).start()

    for k in range(3):
        a_x(0, k).start()
    begin(0)
    for k in range(3):
        a_x(1, k).start()
    for k in range(3):
        w_y(k).start()
    w_own().start()

    PB[...] = jnp.zeros_like(PB)
    acc[...] = jnp.zeros_like(acc)
    for h in range(HEADS):
        gain_rows[h] = gain[h:h + 1].astype(F32)
    row = lax.broadcasted_iota(jnp.int32, (80, 256), 0)
    lane = lax.broadcasted_iota(jnp.int32, (80, 256), 1)
    base = (lane >> 7) * 40 + ((lane >> 6) & 1) * 20
    r16 = lane & 15
    for xx in range(X):
        here = ((lane >> 4) & 3) == xx
        PB[0, xx, 176:256] = jnp.where(here & (row == base + r16), 1.0, 0.0).astype(BF)
        PB[1, xx, 176:256] = jnp.where(here & (row == base + 16 + (r16 & 3)), 1.0, 0.0).astype(BF)

    fetch.wait()
    lane_j = (lax.broadcasted_iota(jnp.int32, (SPAN, E), 1) & 15) >> 2

    def arrange(m, _):
        window = jnp.minimum(lax.div(80 * m, 128), 3)
        off = pl.multiple_of(176 - (80 * m - 128 * window), 16)
        lhs = jnp.concatenate(
            [tokens[:, pl.ds(pl.multiple_of(640 * xx + 128 * window, 128), 256)] for xx in range(X)], axis=1
        )
        first = dot(lhs, jnp.concatenate([PB[0, xx, pl.ds(off, 256)] for xx in range(X)], axis=0)).astype(BF)
        rest = dot(lhs, jnp.concatenate([PB[1, xx, pl.ds(off, 256)] for xx in range(X)], axis=0))
        for half in range(2):
            T1[2 * m + half] = first[:, half * E:(half + 1) * E]
            part = rest[:, half * E:(half + 1) * E]
            for j in range(4):
                T2[j, 2 * m + half] = jnp.where(lane_j == j, part, 0.0).astype(BF)
        return 0

    lax.fori_loop(0, Z // 2, arrange, 0, unroll=2)

    def M(ph, *ds):
        at_z = [zz(d) for d in ds]
        for d in ds:
            to_sibling(ph, d).wait_recv()

        def column(t):
            return jnp.concatenate([G[ph][:, b, :, t].reshape(E, E) for b in at_z], axis=0)

        def rows(j):
            return jnp.concatenate([T1[b] for b in at_z] + [T2[j, b] for b in at_z], axis=1)

        for i in range(WIDE[ph]):
            u, j, t = i // 4, i % 4, FIRST[ph] + i
            if u == 0 and i + 4 < min(WIDE[ph], 8):
                top = jnp.concatenate([column(i), column(i + 4)], axis=1)
                low = jnp.concatenate([column(WIDE[ph]), column(WIDE[ph] + 1)], axis=1)
                both = dot(rows(j), jnp.concatenate([top, low], axis=0))
                acc[t] += both[:, :E]
                acc[t + 4] += both[:, E:]
            elif u != 1:
                acc[t] += dot(rows(j), jnp.concatenate([column(i), column(WIDE[ph] + u)], axis=0))

    AX(0)
    B(0, 1, -1)
    B(0, 3, -3)
    F(0, 0)
    A(0, 1, -1)
    F(0, 1, -1)
    A(0, 3, -3)
    F(0, 3, -3)
    S(0, 0, 1, -1)
    B(0, 6, -6)
    B(0, 2, -2, 4, -4)
    S(0, 3, -3)
    M(0, 1, -1, 3, -3)
    A(0, 6, -6)
    F(0, 6, -6)
    F(0, 2, -2, 4, -4)
    A(0, 2, -2, 4, -4)
    B(0, 5, -5, 7, -7, 8)
    onward(1, 0, b_z)
    AX(1)
    S(0, 2, -2, 4, -4)
    BZ(1, 1, -1)
    BZ(1, 3, -3)
    M(0, 2, -2, 4, -4)
    S(0, 6, -6)
    A(0, 5, -5, 7, -7, 8)
    A(1, 1, -1)
    A(1, 3, -3)
    M(0, 0, 6, -6)
    S(0, 5, -5)
    BZ(1, 6, -6)
    BZ(1, 2, -2, 4, -4)
    S(0, 7, -7, 8)
    BX(1, 0, 1, -1, 3, -3)
    M(0, 5, -5, 7, -7, 8)

    def tile(t):
        return acc[t]

    def silu(v):
        return v / (1.0 + jnp.exp(-v))

    for h in range(HEADS):
        kvq[h] = silu(tile(h)).astype(BF)
        kvq[HEADS + h] = tile(HEADS + h).astype(BF)
        s = lax.dot_general(kvq[h], kvq[HEADS + h], (((0,), (0,)), ((), ())), preferred_element_type=F32)
        state[pl.ds(8 * h, 8)] = s.astype(BF).reshape(8, 16, E)
    pair1 = rcopy(state, sib_state, ps, pr, sibling)
    pair1.start()
    BX(1, 6, -6, 2, -2, 4, -4)
    A(1, 6, -6)
    A(1, 2, -2, 4, -4)
    pair1.wait_recv()
    mine = pl.ds(20 * c, 20)
    chip_sum[...] = (state[mine].astype(F32) + sib_state[mine].astype(F32)).astype(BF)

    def owner_z(i):
        return (i * Z) // OWNERS

    def z1(i):
        dst = owner_z(i)
        return rcopy(
            chip_sum.at[pl.ds(SHARE * i, SHARE)], zin.at[z], z1s, z1r.at[z],
            (y, (x * Z + dst) * 2 + c),
        )

    my_i = lax.div(z * OWNERS + Z - 1, Z)
    is_owner = lax.div(my_i * Z, OWNERS) == z
    for i in range(OWNERS):
        @pl.when(z != owner_z(i))
        def _():
            z1(i).start()

        @pl.when(z == owner_z(i))
        def _():
            zin[z] = chip_sum[pl.ds(SHARE * i, SHARE)]

    BZ(1, 5, -5, 7, -7, 8)
    BX(1, 5, -5, 7, -7, 8)
    F(1, 0, 1, -1, 3, -3)

    def x_copy(k):
        return rcopy(xout, xin.at[x], xs.at[k], xr.at[k], at(dx=XD[k]))

    def z1_in(src):
        return rcopy(chip_sum.at[pl.ds(0, SHARE)], zin.at[src], z1s, z1r.at[src], sibling)

    def z2(dst):
        return rcopy(
            pout.at[dst], pfull.at[pl.ds(20 * c + SHARE * my_i, SHARE)], z2s, z2r.at[my_i],
            (y, (x * Z + dst) * 2 + c),
        )

    def z2_in(i):
        return rcopy(pout.at[0], pfull.at[pl.ds(20 * c + SHARE * i, SHARE)], z2s, z2r.at[i], sibling)

    @pl.when(is_owner)
    def _():
        for src in range(Z):
            @pl.when(src != z)
            def _():
                z1_in(src).wait_recv()
        total = jnp.zeros((SHARE, 16, E), F32)
        for src in range(Z):
            total = total + zin[src].astype(F32)
        xout[...] = total
        for k in range(3):
            x_copy(k).start()

    S(1, 0, 1, -1, 3, -3)
    F(1, 6, -6, 2, -2, 4, -4)
    M(1, 1, -1, 3, -3)

    @pl.when(is_owner)
    def _():
        for k in range(3):
            x_copy(k).wait_recv()
        running = jnp.zeros((SHARE, 16, E), F32)
        for src in range(X):
            running = running + jnp.where((src < x), xin[src], 0.0)
        for dst in range(Z):
            pout[dst] = running.astype(BF)
            running = running + zin[dst].astype(F32)

            @pl.when(dst != z)
            def _():
                z2(dst).start()
        pfull[pl.ds(20 * c + SHARE * my_i, SHARE)] = pout[z]

    S(1, 2, -2, 4, -4)
    S(1, 6, -6)
    A(1, 5, -5, 7, -7, 8)
    S(1, 5, -5, 7, -7, 8)
    M(1, 2, -2, 4, -4)
    M(1, 0, 6, -6)
    M(1, 5, -5, 7, -7, 8)
    for k in range(3):
        w_y(k).wait_recv()
        w_s(k).start()
    w_own().wait()
    for h in range(HEADS):
        kvq[2 * HEADS + h] = silu(tile(2 * HEADS + h)).astype(BF)
    causal = lax.broadcasted_iota(jnp.int32, (SPAN, SPAN), 0) >= lax.broadcasted_iota(jnp.int32, (SPAN, SPAN), 1)
    for h in range(HEADS):
        q, k, v = kvq[2 * HEADS + h], kvq[h], kvq[HEADS + h]
        scores = lax.dot_general(q, k, (((1,), (1,)), ((), ())), preferred_element_type=F32)
        local[h] = dot(jnp.where(causal, scores, 0.0).astype(BF), v)

    def a_y(k, n, h):
        ref = att.at[y, h]
        return rcopy(ref, ref, ats.at[k], atr.at[c if k == 0 else 1 - c, n], at(dy=XD[k]))

    def a_y_on(n):
        ref = att.at[lax.rem(y - way + Y, Y), nth(n)]
        return rcopy(ref, ref, ats.at[2], atr.at[2, n], at(dy=way))

    def a_y_in(kind, n):
        return rcopy(att.at[y, 0], att.at[y, 0], ats.at[0], atr.at[kind, n], sibling)

    def nth(n):
        return lax.rem(n + 3 * c, HEADS)

    def pair2(n):
        first, size = (4 * c, 8) if n == 0 else ((4 * c + 8, 8) if n == 1 else (16 * (1 - c), 4))
        ref = pfull.at[pl.ds(20 * c + first, size)]
        return rcopy(ref, ref, qs.at[n], qr.at[n], sibling)

    def combine(n):
        h = nth(n)
        before = pfull[pl.ds(8 * h, 8)].reshape(E, E).astype(F32)
        first = sib_state[pl.ds(8 * h, 8)].reshape(E, E).astype(F32)
        prefix = jnp.where(c == 1, before + first, before).astype(BF)
        combined = dot(kvq[2 * HEADS + h], prefix) + local[h]
        scale = lax.rsqrt(jnp.mean(combined * combined, axis=-1, keepdims=True) + 1e-05)
        att[y, h] = (combined * scale * gain_rows[h]).astype(BF)
        for k in range(2):
            a_y(k, n, h).start()

    for n, order in enumerate(((0, 1, 2, 3), (4, 5, 6, 7), (8, 9))):
        for i in order:
            i = lax.rem(i + 2 * c, OWNERS)

            @pl.when(z != lax.div(i * Z, OWNERS))
            def _():
                z2_in(i).wait_recv()
        pair2(n).start()
        if n < 2:
            combine(n)
    for n in range(3):
        pair2(n).wait_recv()
    for n in range(2, HEADS):
        combine(n)

    def project(section):
        lhs = jnp.concatenate([att[section, h] for h in range(HEADS)], axis=1)
        return dot(lhs, wo[section])

    for k in range(3):
        w_s(k).wait_recv()
    total = tokens[:, pl.ds(pl.multiple_of(640 * y, 128), 640)].astype(F32) + project(y)
    for n in range(HEADS):
        a_y_in(0, n).wait_recv()
        a_y_on(n).start()
    total = total + project(lax.rem(y - way + Y, Y))

    for k in range(3):
        w_y(k).wait_send()
        w_s(k).wait_send()

    def sent(ref, sem):
        rcopy(ref, ref, sem, sem, sibling).wait_send()

    for ph in range(2):
        sent(G[ph].at[c, z, pl.ds(0, 3), part_a(ph)], axs.at[ph])
        sent(G[ph].at[c, pl.ds(0, Z - 1), :, part_a(ph)], azs.at[ph])
        sent(G[ph].at[c, pl.ds(0, Z - 1), x, part_b(ph)], bzs.at[ph])
        sent(G[ph].at[c, :, pl.ds(0, 3), part_b(ph)], bxs.at[ph])
        sent(G[ph].at[c], ss.at[ph])
    pair1.wait_send()
    for n in range(3):
        pair2(n).wait_send()
    @pl.when(is_owner)
    def _():
        sent(chip_sum.at[pl.ds(0, SHARE * (OWNERS - 1))], z1s)
        sent(pout.at[pl.ds(0, Z - 1)], z2s)
        for k in range(3):
            x_copy(k).wait_send()

    @pl.when(jnp.logical_not(is_owner))
    def _():
        sent(chip_sum, z1s)

    for kind, section in ((1, y + way), (2, y + 2)):
        for n in range(HEADS):
            a_y_in(kind, n).wait_recv()
        total = total + project(lax.rem(section + Y, Y))
    out[...] = total.astype(BF)
    for k in range(3):
        sent(att.at[0], ats.at[k])


def on_device(tokens, w_query, w_key, w_value, gain, w_out):
    vmem = pl.BlockSpec(memory_space=pltpu.VMEM)
    hbm = pl.BlockSpec(memory_space=pl.ANY)
    dma = pltpu.SemaphoreType.DMA
    return pl.pallas_call(
        kernel,
        name="layer",
        out_shape=jax.ShapeDtypeStruct((SPAN, 640), BF),
        in_specs=[hbm, vmem, vmem, vmem, vmem, hbm],
        out_specs=vmem,
        scratch_shapes=[
            pltpu.VMEM((SPAN, 2560), BF),
            pltpu.VMEM((HEADS, 1, E), F32),
            pltpu.VMEM((2, Z, X, TILES[0], 16, E), BF),
            pltpu.VMEM((2, Z, X, TILES[1], 16, E), BF),
            pltpu.VMEM((Z, SPAN, E), BF),
            pltpu.VMEM((4, Z, SPAN, E), BF),
            pltpu.VMEM((2, X, 432, 256), BF),
            pltpu.VMEM((COLS, SPAN, E), F32),
            pltpu.VMEM((Y, 640, 640), BF),
            pltpu.VMEM((COLS, SPAN, E), BF),
            pltpu.VMEM((HEADS, SPAN, E), F32),
            pltpu.VMEM((Y, HEADS, SPAN, E), BF),
            pltpu.VMEM((40, 16, E), BF),
            pltpu.VMEM((40, 16, E), BF),
            pltpu.VMEM((20, 16, E), BF),
            pltpu.VMEM((Z, SHARE, 16, E), BF),
            pltpu.VMEM((SHARE, 16, E), F32),
            pltpu.VMEM((X, SHARE, 16, E), F32),
            pltpu.VMEM((Z, SHARE, 16, E), BF),
            pltpu.VMEM((40, 16, E), BF),
            dma((2,)), dma((2,)),
            dma((2,)), dma((2, Z)),
            dma((2,)), dma((2, Z)),
            dma((2,)), dma((2, Z, 2)),
            dma((2,)), dma((2, Z)),
            dma((3,)), dma((3,)), dma((3,)), dma((3,)), dma(()),
            dma(()), dma(()),
            dma(()), dma((Z,)),
            dma((3,)), dma((3,)),
            dma(()), dma((OWNERS,)),
            dma((3,)), dma((3,)),
            dma((3,)), dma((3, HEADS)), dma(()),
        ],
        compiler_params=pltpu.CompilerParams(
            collective_id=1, has_side_effects=True, vmem_limit_bytes=56 << 20
        ),
    )(tokens, w_query, w_key, w_value, gain.reshape(HEADS, E), w_out)


def solution(mesh):
    placed = (
        P("seq", None),
        P("seq", "section"),
        P("seq", "section"),
        P("seq", "section"),
        P("section"),
        P("section", None),
    )
    return jax.shard_map(
        on_device, mesh=mesh, in_specs=placed, out_specs=P("seq", "section"), check_vma=False
    )
```

```python
import jax
import jax.numpy as jnp
from jax import lax
from jax.experimental import pallas as pl
from jax.experimental.pallas import tpu as pltpu
from jax.sharding import PartitionSpec as P

E = 128
X, Z, Y = 4, 16, 4
ROWS = 20
HEADS = 5
COLS = 3 * HEADS
FIRST = (0, 2 * HEADS)
WIDE = (2 * HEADS, HEADS)
TILES = (13, 7)
CUT = (2, 2)
SPAN = 256
OWNERS, SHARE = 10, 2
MESH = pl.DeviceIdType.MESH
BF = jnp.bfloat16
F32 = jnp.float32


def dot(a, b):
    return jnp.dot(a, b, preferred_element_type=F32)


def kernel(
    tokens_hbm, wq, wk, wv, gain, w_out, out, tokens,
    gain_rows, G0, G1, T1, T2, PB, acc, wo, kvq, local, att,
    state, sib_state, chip_sum, zin, xout, xin, pout, pfull,
    axs, axr, azs, azr, bzs, bzr, bxs, bxr, ss, sr,
    ws, wr, vs, vr, wl, ps, pr, z1s, z1r, xs, xr, z2s, z2r, qs, qr, ats, atr, tl,
):
    seq = lax.axis_index("seq")
    y = lax.axis_index("section")
    c = lax.rem(seq, 2)
    z = lax.rem(lax.div(seq, 2), Z)
    x = lax.div(seq, 2 * Z)

    def at(dx=0, dy=0, dz=0, core=None):
        core = c if core is None else core
        nx, ny, nz = lax.rem(x + dx + X, X), lax.rem(y + dy + Y, Y), lax.rem(z + dz + Z, Z)
        return (ny, (nx * Z + nz) * 2 + core)

    def zz(d):
        return lax.rem(z + d + Z, Z)

    def rcopy(src, dst, ssem, rsem, dev):
        return pltpu.make_async_remote_copy(
            src_ref=src, dst_ref=dst, send_sem=ssem, recv_sem=rsem,
            device_id=dev, device_id_type=MESH,
        )

    sibling = at(core=1 - c)

    way = 1 - 2 * c
    G = (G0, G1)

    barrier = pltpu.get_barrier_semaphore()
    greeted = [at(dz=d) for d in (1, -1, 2, -2, 3, -3)] + [at(dx=1), at(dx=-1), at(dx=2), sibling]
    greeted += [at(dy=1), at(dy=-1), at(dy=2)]
    for dev in greeted:
        pl.semaphore_signal(barrier, inc=1, device_id=dev, device_id_type=MESH)
    fetch = pltpu.make_async_copy(tokens_hbm, tokens, tl)
    fetch.start()

    weights = (wk, wv, wq)
    for ph in range(2):
        for i in range(WIDE[ph]):
            t = FIRST[ph] + i
            G[ph][c, z, x, i] = weights[t // HEADS][0:16, pl.ds((t % HEADS) * E, E)]
        for u in range(TILES[ph] - WIDE[ph]):
            parts = []
            for i in range(4 * u, 4 * u + 4):
                t = FIRST[ph] + i
                if i < WIDE[ph]:
                    parts.append(weights[t // HEADS][16:20, pl.ds((t % HEADS) * E, E)].astype(F32))
                else:
                    parts.append(jnp.zeros((4, E), F32))
            G[ph][c, z, x, WIDE[ph] + u] = jnp.concatenate(parts, axis=0).astype(BF)

    pl.semaphore_wait(barrier, len(greeted))

    XD = (1, -1, 2)

    def place(d):
        return (d + 7) % Z

    def part_a(ph):
        return pl.ds(0, CUT[ph])

    def part_b(ph):
        return pl.ds(CUT[ph], TILES[ph] - CUT[ph])

    def a_x(ph, k):
        ref = G[ph].at[c, z, x, part_a(ph)]
        return rcopy(ref, ref, axs.at[ph], axr.at[ph], at(dx=XD[k]))

    def a_x_in(ph):
        ref = G[ph].at[c, z, pl.ds(0, 3), part_a(ph)]
        return rcopy(ref, ref, axs.at[ph], axr.at[ph], sibling)

    def a_z(ph, d, delta):
        ref = G[ph].at[c, zz(d), :, part_a(ph)]
        return rcopy(ref, ref, azs.at[ph], azr.at[ph, place(d - delta)], at(dz=delta))

    def b_z(ph, d, delta):
        ref = G[ph].at[c, zz(d), x, part_b(ph)]
        return rcopy(ref, ref, bzs.at[ph], bzr.at[ph, place(d - delta)], at(dz=delta))

    def opposite(copy_of, ph):
        ref = copy_of(ph, zz(-6 * way))
        sems = (azs, azr) if copy_of is ref_a else (bzs, bzr)
        return rcopy(ref, ref, sems[0].at[ph], sems[1].at[ph, place(8)], at(dz=2 * way))

    def ref_a(ph, block):
        return G[ph].at[c, block, :, part_a(ph)]

    def ref_b(ph, block):
        return G[ph].at[c, block, x, part_b(ph)]

    def late(d):
        return abs(d) in (5, 7, 8)

    def b_x(ph, d, k):
        ref = ref_b(ph, zz(d))
        kind = 1 if late(d) else (c if k == 0 else 1 - c)
        return rcopy(ref, ref, bxs.at[ph], bxr.at[ph, place(d), kind], at(dx=XD[k]))

    def b_x_on(ph, d):
        ref = G[ph].at[c, zz(d), lax.rem(x - way + X, X), part_b(ph)]
        return rcopy(ref, ref, bxs.at[ph], bxr.at[ph, place(d), 1], at(dx=way))

    def b_x_in(ph, d, kind, count):
        ref = G[ph].at[c, zz(d), pl.ds(0, count), part_b(ph)]
        return rcopy(ref, ref, bxs.at[ph], bxr.at[ph, place(d), kind], sibling)

    def to_sibling(ph, d):
        ref = G[ph].at[c, zz(d)]
        return rcopy(ref, ref, ss.at[ph], sr.at[ph, place(d)], sibling)

    def onward(ph, d, copy):
        jumps = {0: (3, -3, 1, -1), 3: (-3, -1, 1), 6: (-1, 1)}.get(abs(d), ())
        for jump in jumps:
            copy(ph, d, jump if d >= 0 else -jump).start()

    def A(ph, *ds):
        for d in ds:
            ref = ref_a(ph, zz(d))
            rcopy(ref, ref, azs.at[ph], azr.at[ph, place(d)], sibling).wait_recv()
            onward(ph, d, a_z)
        if 6 in ds:
            opposite(ref_a, ph).start()

    def BZ(ph, *ds):
        for d in ds:
            ref = ref_b(ph, zz(d))
            rcopy(ref, ref, bzs.at[ph], bzr.at[ph, place(d)], sibling).wait_recv()
            onward(ph, d, b_z)
        if 6 in ds:
            opposite(ref_b, ph).start()

    def BX(ph, *ds):
        for d in ds:
            for k in (2, 0, 1) if late(d) else (0, 1):
                b_x(ph, d, k).start()

    def B(ph, *ds):
        BZ(ph, *ds)
        BX(ph, *ds)

    def F(ph, *ds):
        for d in ds:
            b_x_in(ph, d, 0, 1).wait_recv()
            b_x_on(ph, d).start()

    def S(ph, *ds):
        for d in ds:
            b_x_in(ph, d, 1, 3 if late(d) else 2).wait_recv()
            to_sibling(ph, d).start()

    def AX(ph):
        a_x_in(ph).wait_recv()
        onward(ph, 0, a_z)

    def w_y(k):
        dev = at(dy=XD[k])
        return rcopy(
            w_out.at[pl.ds(320 * c, 320), pl.ds(pl.multiple_of(640 * dev[0], 128), 640)],
            wo.at[y, pl.ds(320 * c, 320)], ws.at[k], wr.at[k], dev,
        )

    def w_s(k):
        ref = wo.at[lax.rem(y - XD[k] + Y, Y), pl.ds(320 * c, 320)]
        return rcopy(ref, ref, vs.at[k], vr.at[k], sibling)

    def w_own():
        return pltpu.make_async_copy(
            w_out.at[:, pl.ds(pl.multiple_of(640 * y, 128), 640)], wo.at[y], wl
        )

    def begin(ph):
        onward(ph, 0, b_z)
        for k in range(2):
            b_x(ph, 0, k).start()

    for k in range(3):
        a_x(0, k).start()
    begin(0)
    for k in range(3):
        a_x(1, k).start()
    for k in range(3):
        w_y(k).start()
    w_own().start()

    PB[...] = jnp.zeros_like(PB)
    acc[...] = jnp.zeros_like(acc)
    for h in range(HEADS):
        gain_rows[h] = gain[h:h + 1].astype(F32)
    row = lax.broadcasted_iota(jnp.int32, (80, 256), 0)
    lane = lax.broadcasted_iota(jnp.int32, (80, 256), 1)
    base = (lane >> 7) * 40 + ((lane >> 6) & 1) * 20
    r16 = lane & 15
    for xx in range(X):
        here = ((lane >> 4) & 3) == xx
        PB[0, xx, 176:256] = jnp.where(here & (row == base + r16), 1.0, 0.0).astype(BF)
        PB[1, xx, 176:256] = jnp.where(here & (row == base + 16 + (r16 & 3)), 1.0, 0.0).astype(BF)

    fetch.wait()
    lane_j = (lax.broadcasted_iota(jnp.int32, (SPAN, E), 1) & 15) >> 2

    def arrange(m, _):
        window = jnp.minimum(lax.div(80 * m, 128), 3)
        off = pl.multiple_of(176 - (80 * m - 128 * window), 16)
        lhs = jnp.concatenate(
            [tokens[:, pl.ds(pl.multiple_of(640 * xx + 128 * window, 128), 256)] for xx in range(X)], axis=1
        )
        first = dot(lhs, jnp.concatenate([PB[0, xx, pl.ds(off, 256)] for xx in range(X)], axis=0)).astype(BF)
        rest = dot(lhs, jnp.concatenate([PB[1, xx, pl.ds(off, 256)] for xx in range(X)], axis=0))
        for half in range(2):
            T1[2 * m + half] = first[:, half * E:(half + 1) * E]
            part = rest[:, half * E:(half + 1) * E]
            for j in range(4):
                T2[j, 2 * m + half] = jnp.where(lane_j == j, part, 0.0).astype(BF)
        return 0

    lax.fori_loop(0, Z // 2, arrange, 0, unroll=2)

    def M(ph, *ds):
        at_z = [zz(d) for d in ds]
        for d in ds:
            to_sibling(ph, d).wait_recv()

        def column(t):
            return jnp.concatenate([G[ph][:, b, :, t].reshape(E, E) for b in at_z], axis=0)

        def rows(j):
            return jnp.concatenate([T1[b] for b in at_z] + [T2[j, b] for b in at_z], axis=1)

        for i in range(WIDE[ph]):
            u, j, t = i // 4, i % 4, FIRST[ph] + i
            if u == 0 and i + 4 < min(WIDE[ph], 8):
                top = jnp.concatenate([column(i), column(i + 4)], axis=1)
                low = jnp.concatenate([column(WIDE[ph]), column(WIDE[ph] + 1)], axis=1)
                both = dot(rows(j), jnp.concatenate([top, low], axis=0))
                acc[t] += both[:, :E]
                acc[t + 4] += both[:, E:]
            elif u != 1:
                acc[t] += dot(rows(j), jnp.concatenate([column(i), column(WIDE[ph] + u)], axis=0))

    AX(0)
    B(0, 1, -1)
    B(0, 3, -3)
    F(0, 0)
    A(0, 1, -1)
    F(0, 1, -1)
    A(0, 3, -3)
    F(0, 3, -3)
    S(0, 0, 1, -1)
    B(0, 6, -6)
    B(0, 2, -2, 4, -4)
    S(0, 3, -3)
    M(0, 1, -1, 3, -3)
    A(0, 6, -6)
    F(0, 6, -6)
    F(0, 2, -2, 4, -4)
    A(0, 2, -2, 4, -4)
    B(0, 5, -5, 7, -7, 8)
    onward(1, 0, b_z)
    AX(1)
    S(0, 2, -2, 4, -4)
    BZ(1, 1, -1)
    BZ(1, 3, -3)
    M(0, 2, -2, 4, -4)
    S(0, 6, -6)
    A(0, 5, -5, 7, -7, 8)
    A(1, 1, -1)
    A(1, 3, -3)
    M(0, 0, 6, -6)
    S(0, 5, -5)
    BZ(1, 6, -6)
    BZ(1, 2, -2, 4, -4)
    S(0, 7, -7, 8)
    BX(1, 0, 1, -1, 3, -3)
    M(0, 5, -5, 7, -7, 8)

    def tile(t):
        return acc[t]

    def silu(v):
        return v / (1.0 + jnp.exp(-v))

    for h in range(HEADS):
        kvq[h] = silu(tile(h)).astype(BF)
        kvq[HEADS + h] = tile(HEADS + h).astype(BF)
        s = lax.dot_general(kvq[h], kvq[HEADS + h], (((0,), (0,)), ((), ())), preferred_element_type=F32)
        state[pl.ds(8 * h, 8)] = s.astype(BF).reshape(8, 16, E)
    pair1 = rcopy(state, sib_state, ps, pr, sibling)
    pair1.start()
    BX(1, 6, -6, 2, -2, 4, -4)
    A(1, 6, -6)
    A(1, 2, -2, 4, -4)
    pair1.wait_recv()
    mine = pl.ds(20 * c, 20)
    chip_sum[...] = (state[mine].astype(F32) + sib_state[mine].astype(F32)).astype(BF)

    def owner_z(i):
        return (i * Z) // OWNERS

    def z1(i):
        dst = owner_z(i)
        return rcopy(
            chip_sum.at[pl.ds(SHARE * i, SHARE)], zin.at[z], z1s, z1r.at[z],
            (y, (x * Z + dst) * 2 + c),
        )

    my_i = lax.div(z * OWNERS + Z - 1, Z)
    is_owner = lax.div(my_i * Z, OWNERS) == z
    for i in range(OWNERS):
        @pl.when(z != owner_z(i))
        def _():
            z1(i).start()

        @pl.when(z == owner_z(i))
        def _():
            zin[z] = chip_sum[pl.ds(SHARE * i, SHARE)]

    BZ(1, 5, -5, 7, -7, 8)
    BX(1, 5, -5, 7, -7, 8)
    F(1, 0, 1, -1, 3, -3)

    def x_copy(k):
        return rcopy(xout, xin.at[x], xs.at[k], xr.at[k], at(dx=XD[k]))

    def z1_in(src):
        return rcopy(chip_sum.at[pl.ds(0, SHARE)], zin.at[src], z1s, z1r.at[src], sibling)

    def z2(dst):
        return rcopy(
            pout.at[dst], pfull.at[pl.ds(20 * c + SHARE * my_i, SHARE)], z2s, z2r.at[my_i],
            (y, (x * Z + dst) * 2 + c),
        )

    def z2_in(i):
        return rcopy(pout.at[0], pfull.at[pl.ds(20 * c + SHARE * i, SHARE)], z2s, z2r.at[i], sibling)

    @pl.when(is_owner)
    def _():
        for src in range(Z):
            @pl.when(src != z)
            def _():
                z1_in(src).wait_recv()
        total = jnp.zeros((SHARE, 16, E), F32)
        for src in range(Z):
            total = total + zin[src].astype(F32)
        xout[...] = total
        for k in range(3):
            x_copy(k).start()

    S(1, 0, 1, -1, 3, -3)
    F(1, 6, -6, 2, -2, 4, -4)
    M(1, 1, -1, 3, -3)

    @pl.when(is_owner)
    def _():
        for k in range(3):
            x_copy(k).wait_recv()
        running = jnp.zeros((SHARE, 16, E), F32)
        for src in range(X):
            running = running + jnp.where((src < x), xin[src], 0.0)
        for dst in range(Z):
            pout[dst] = running.astype(BF)
            running = running + zin[dst].astype(F32)
        for d in (8, 7, 9, 6, 10, 5, 11, 4, 12, 3, 13, 2, 14, 1, 15):
            z2(zz(d)).start()
        pfull[pl.ds(20 * c + SHARE * my_i, SHARE)] = pout[z]

    S(1, 2, -2, 4, -4)
    S(1, 6, -6)
    A(1, 5, -5, 7, -7, 8)
    S(1, 5, -5, 7, -7, 8)
    M(1, 2, -2, 4, -4)
    M(1, 0, 6, -6)
    M(1, 5, -5, 7, -7, 8)
    for k in range(3):
        w_y(k).wait_recv()
        w_s(k).start()
    w_own().wait()
    for h in range(HEADS):
        kvq[2 * HEADS + h] = silu(tile(2 * HEADS + h)).astype(BF)
    causal = lax.broadcasted_iota(jnp.int32, (SPAN, SPAN), 0) >= lax.broadcasted_iota(jnp.int32, (SPAN, SPAN), 1)
    for h in range(HEADS):
        q, k, v = kvq[2 * HEADS + h], kvq[h], kvq[HEADS + h]
        scores = lax.dot_general(q, k, (((1,), (1,)), ((), ())), preferred_element_type=F32)
        local[h] = dot(jnp.where(causal, scores, 0.0).astype(BF), v)

    def a_y(k, n, h):
        ref = att.at[y, h]
        return rcopy(ref, ref, ats.at[k], atr.at[c if k == 0 else 1 - c, n], at(dy=XD[k]))

    def a_y_on(n):
        ref = att.at[lax.rem(y - way + Y, Y), nth(n)]
        return rcopy(ref, ref, ats.at[2], atr.at[2, n], at(dy=way))

    def a_y_in(kind, n):
        return rcopy(att.at[y, 0], att.at[y, 0], ats.at[0], atr.at[kind, n], sibling)

    def nth(n):
        return lax.rem(n + 3 * c, HEADS)

    def pair2(n):
        first, size = (4 * c, 8) if n == 0 else ((4 * c + 8, 8) if n == 1 else (16 * (1 - c), 4))
        ref = pfull.at[pl.ds(20 * c + first, size)]
        return rcopy(ref, ref, qs.at[n], qr.at[n], sibling)

    def combine(n):
        h = nth(n)
        before = pfull[pl.ds(8 * h, 8)].reshape(E, E).astype(F32)
        first = sib_state[pl.ds(8 * h, 8)].reshape(E, E).astype(F32)
        prefix = jnp.where(c == 1, before + first, before).astype(BF)
        combined = dot(kvq[2 * HEADS + h], prefix) + local[h]
        scale = lax.rsqrt(jnp.mean(combined * combined, axis=-1, keepdims=True) + 1e-05)
        att[y, h] = (combined * scale * gain_rows[h]).astype(BF)
        for k in range(2):
            a_y(k, n, h).start()

    for n, order in enumerate(((0, 1, 2, 3), (4, 5, 6, 7), (8, 9))):
        for i in order:
            i = lax.rem(i + 2 * c, OWNERS)

            @pl.when(z != lax.div(i * Z, OWNERS))
            def _():
                z2_in(i).wait_recv()
        pair2(n).start()
        if n < 2:
            combine(n)
    for n in range(3):
        pair2(n).wait_recv()
    for n in range(2, HEADS):
        combine(n)

    def project(section):
        lhs = jnp.concatenate([att[section, h] for h in range(HEADS)], axis=1)
        return dot(lhs, wo[section])

    for k in range(3):
        w_s(k).wait_recv()
    total = tokens[:, pl.ds(pl.multiple_of(640 * y, 128), 640)].astype(F32) + project(y)
    for n in range(HEADS):
        a_y_in(0, n).wait_recv()
        a_y_on(n).start()
    total = total + project(lax.rem(y - way + Y, Y))

    for k in range(3):
        w_y(k).wait_send()
        w_s(k).wait_send()

    def sent(ref, sem):
        rcopy(ref, ref, sem, sem, sibling).wait_send()

    for ph in range(2):
        sent(G[ph].at[c, z, pl.ds(0, 3), part_a(ph)], axs.at[ph])
        sent(G[ph].at[c, pl.ds(0, Z - 1), :, part_a(ph)], azs.at[ph])
        sent(G[ph].at[c, pl.ds(0, Z - 1), x, part_b(ph)], bzs.at[ph])
        sent(G[ph].at[c, :, pl.ds(0, 3), part_b(ph)], bxs.at[ph])
        sent(G[ph].at[c], ss.at[ph])
    pair1.wait_send()
    for n in range(3):
        pair2(n).wait_send()
    @pl.when(is_owner)
    def _():
        sent(chip_sum.at[pl.ds(0, SHARE * (OWNERS - 1))], z1s)
        sent(pout.at[pl.ds(0, Z - 1)], z2s)
        for k in range(3):
            x_copy(k).wait_send()

    @pl.when(jnp.logical_not(is_owner))
    def _():
        sent(chip_sum, z1s)

    for kind, section in ((1, y + way), (2, y + 2)):
        for n in range(HEADS):
            a_y_in(kind, n).wait_recv()
        total = total + project(lax.rem(section + Y, Y))
    out[...] = total.astype(BF)
    for k in range(3):
        sent(att.at[0], ats.at[k])


def on_device(tokens, w_query, w_key, w_value, gain, w_out):
    vmem = pl.BlockSpec(memory_space=pltpu.VMEM)
    hbm = pl.BlockSpec(memory_space=pl.ANY)
    dma = pltpu.SemaphoreType.DMA
    return pl.pallas_call(
        kernel,
        name="layer",
        out_shape=jax.ShapeDtypeStruct((SPAN, 640), BF),
        in_specs=[hbm, vmem, vmem, vmem, vmem, hbm],
        out_specs=vmem,
        scratch_shapes=[
            pltpu.VMEM((SPAN, 2560), BF),
            pltpu.VMEM((HEADS, 1, E), F32),
            pltpu.VMEM((2, Z, X, TILES[0], 16, E), BF),
            pltpu.VMEM((2, Z, X, TILES[1], 16, E), BF),
            pltpu.VMEM((Z, SPAN, E), BF),
            pltpu.VMEM((4, Z, SPAN, E), BF),
            pltpu.VMEM((2, X, 432, 256), BF),
            pltpu.VMEM((COLS, SPAN, E), F32),
            pltpu.VMEM((Y, 640, 640), BF),
            pltpu.VMEM((COLS, SPAN, E), BF),
            pltpu.VMEM((HEADS, SPAN, E), F32),
            pltpu.VMEM((Y, HEADS, SPAN, E), BF),
            pltpu.VMEM((40, 16, E), BF),
            pltpu.VMEM((40, 16, E), BF),
            pltpu.VMEM((20, 16, E), BF),
            pltpu.VMEM((Z, SHARE, 16, E), BF),
            pltpu.VMEM((SHARE, 16, E), F32),
            pltpu.VMEM((X, SHARE, 16, E), F32),
            pltpu.VMEM((Z, SHARE, 16, E), BF),
            pltpu.VMEM((40, 16, E), BF),
            dma((2,)), dma((2,)),
            dma((2,)), dma((2, Z)),
            dma((2,)), dma((2, Z)),
            dma((2,)), dma((2, Z, 2)),
            dma((2,)), dma((2, Z)),
            dma((3,)), dma((3,)), dma((3,)), dma((3,)), dma(()),
            dma(()), dma(()),
            dma(()), dma((Z,)),
            dma((3,)), dma((3,)),
            dma(()), dma((OWNERS,)),
            dma((3,)), dma((3,)),
            dma((3,)), dma((3, HEADS)), dma(()),
        ],
        compiler_params=pltpu.CompilerParams(
            collective_id=1, has_side_effects=True, vmem_limit_bytes=56 << 20
        ),
    )(tokens, w_query, w_key, w_value, gain.reshape(HEADS, E), w_out)


def solution(mesh):
    placed = (
        P("seq", None),
        P("seq", "section"),
        P("seq", "section"),
        P("seq", "section"),
        P("section"),
        P("section", None),
    )
    return jax.shard_map(
        on_device, mesh=mesh, in_specs=placed, out_specs=P("seq", "section"), check_vma=False
    )
```
